128 devices in a mesh: chain: 8 (over x, z_lo), op: 16 (over y, z_hi, core).
Axes of the slice: x: 4, y: 4, z: 4 (z_hi: 2, z_lo: 2; z = z_hi * 2 + z_lo), core: 2. Of those that a mesh axis runs over, the one named last changes fastest.
Arguments:
- env_in: bfloat16 [16, 16, 128, 128], P('op'), may hold values from -6 to 6
- mps: bfloat16 [8, 4, 16, 128, 128], P('chain'), may hold values from -0.5 to 0.5
- proj: bfloat16 [8, 4, 16, 128, 128], P('chain'), may hold values from -0.5 to 0.5
- mpo: bfloat16 [8, 16, 4, 16, 4], P('chain'), may hold values from -2 to 2
- mpo_charge: int32 [16, 2], replicated, may hold values from -1 to 1
- block_sizes: int32 [9, 16], replicated, may hold values from 32 to 128
Outputs:
- env_out: bfloat16 [8, 16, 16, 128, 128], P('chain', 'op')
The draws below stay inside these ranges and needn't reach their ends.
All inputs are finite; a program needn't handle non-finite values.
Results may differ from the reference program's by a relative error of at most 0.025.
Values may be sent and summed in bfloat16 or wider, within the bound.
A program may use at most 64 MiB of HBM per device.

```python
import jax
import jax.numpy as jnp
from jax import lax

MPO_BOND = 16
BLOCK_DIM = 128
UP_VALUES = 8
DOWN_VALUES = 2
SECTORS = 16
CHAIN_SITES = 8


def touch_ends(values, key, least, high):
    spot = [jax.random.randint(jax.random.fold_in(key, axis), (), 0, length) for axis, length in enumerate(values.shape)]
    widest = values.shape.index(max(values.shape))
    beside = spot[:widest] + [(spot[widest] + 1) % values.shape[widest]] + spot[widest + 1:]
    return values.at[tuple(spot)].set(least).at[tuple(beside)].set(high)


def block_scale(stream_key, extent, split, low, high):
    level, own = 1.0, jax.random.fold_in(stream_key, 6)
    for position, blocks in split:
        draws = jnp.exp(jax.random.uniform(jax.random.fold_in(own, position), (blocks,), jnp.float32, low / len(split), high / len(split)))
        level = level * jnp.repeat(draws, extent[position] // blocks).reshape([-1 if axis == position else 1 for axis in range(len(extent))])
    return level


def noise(key, dims, deviation, most, split=(), held_as=jnp.bfloat16):
    values = deviation * jax.random.normal(key, dims, jnp.float32)
    if split:
        values = values * block_scale(key, dims, split, -0.22, 0.18)
    return jnp.clip(values, -most, most).astype(held_as)


def setup_inputs(seed: int = 0) -> dict:
    seeds = jax.random.split(jax.random.key(seed), 7)
    env_in = noise(seeds[0], (MPO_BOND, SECTORS, BLOCK_DIM, BLOCK_DIM), 1.0, 6.0, ((0, 16),))
    mps = noise(seeds[1], (CHAIN_SITES, 4, SECTORS, BLOCK_DIM, BLOCK_DIM), BLOCK_DIM ** -0.5, 0.5, ((0, 8),))
    proj = noise(seeds[2], (CHAIN_SITES, 4, SECTORS, BLOCK_DIM, BLOCK_DIM), BLOCK_DIM ** -0.5, 0.5, ((0, 8),))
    mpo = noise(seeds[3], (CHAIN_SITES, MPO_BOND, 4, MPO_BOND, 4), (MPO_BOND // 2) ** -0.5, 2.0, ((0, 8),))
    mpo_charge = touch_ends(jax.random.randint(seeds[4], (MPO_BOND, 2), -1, 2), jax.random.fold_in(seeds[4], 1), -1, 1).astype(jnp.int32)
    block_sizes = touch_ends(jax.random.randint(seeds[5], (CHAIN_SITES + 1, SECTORS), BLOCK_DIM // 4, BLOCK_DIM + 1), jax.random.fold_in(seeds[5], 1), BLOCK_DIM // 4, BLOCK_DIM).astype(jnp.int32)
    return {"env_in": env_in, "mps": mps, "proj": proj, "mpo": mpo, "mpo_charge": mpo_charge, "block_sizes": block_sizes}


UP_CHARGE = (0, 1, 0, 1)
DOWN_CHARGE = (0, 0, 1, 1)


def mask_site(site_mps, site_proj, left_sizes, right_sizes):
    positions = jnp.arange(BLOCK_DIM, dtype=jnp.int32)
    up_index = jnp.arange(UP_VALUES, dtype=jnp.int32)[:, None]
    down_index = jnp.arange(DOWN_VALUES, dtype=jnp.int32)[None, :]
    left_grid = left_sizes.reshape(UP_VALUES, DOWN_VALUES)
    right_grid = jnp.pad(right_sizes.reshape(UP_VALUES, DOWN_VALUES), ((0, 1), (0, 1)))
    mps_grid = site_mps.reshape(4, UP_VALUES, DOWN_VALUES, BLOCK_DIM, BLOCK_DIM)
    proj_grid = site_proj.reshape(4, UP_VALUES, DOWN_VALUES, BLOCK_DIM, BLOCK_DIM)
    mps_parts = []
    proj_parts = []
    for phys_state in range(4):
        up_shift = UP_CHARGE[phys_state]
        down_shift = DOWN_CHARGE[phys_state]
        right_here = right_grid[up_shift:up_shift + UP_VALUES, down_shift:down_shift + DOWN_VALUES]
        row_keep = positions[None, None, :] < left_grid[:, :, None]
        column_keep = positions[None, None, :] < right_here[:, :, None]
        keep_mask = row_keep[:, :, :, None] & column_keep[:, :, None, :]
        mps_parts.append(jnp.where(keep_mask, mps_grid[phys_state], jnp.zeros_like(mps_grid[phys_state])))
        inside = (up_index + up_shift < UP_VALUES) & (down_index + down_shift < DOWN_VALUES)
        proj_parts.append(jnp.where(inside[:, :, None, None], proj_grid[phys_state], jnp.zeros_like(proj_grid[phys_state])))
    return jnp.stack(mps_parts, axis=0), jnp.stack(proj_parts, axis=0)


def mask_mpo(site_mpo, mpo_charge):
    up_state = jnp.array(UP_CHARGE, dtype=jnp.int32)
    down_state = jnp.array(DOWN_CHARGE, dtype=jnp.int32)
    up_bond = mpo_charge[:, 0]
    down_bond = mpo_charge[:, 1]
    match_up = (up_bond[:, None, None, None] + up_state[None, None, None, :]) == (up_state[None, :, None, None] + up_bond[None, None, :, None])
    match_down = (down_bond[:, None, None, None] + down_state[None, None, None, :]) == (down_state[None, :, None, None] + down_bond[None, None, :, None])
    return jnp.where(match_up & match_down, site_mpo, jnp.zeros_like(site_mpo))


def site_step(environment, mps_grid, proj_padded, mpo_masked, mpo_charge):
    env_pad = jnp.pad(environment, ((0, 0), (1, 0), (1, 0), (0, 0), (0, 0)))
    mps_pad = jnp.pad(mps_grid, ((0, 0), (1, 0), (1, 0), (0, 0), (0, 0)))
    pieces = []
    for phys_state in range(4):
        up_shift = UP_CHARGE[phys_state]
        down_shift = DOWN_CHARGE[phys_state]
        env_part = env_pad[:, 1 - up_shift:1 - up_shift + UP_VALUES, 1 - down_shift:1 - down_shift + DOWN_VALUES]
        mps_part = mps_pad[phys_state, 1 - up_shift:1 - up_shift + UP_VALUES, 1 - down_shift:1 - down_shift + DOWN_VALUES]
        product = jnp.einsum('wudab,udbc->wudac', env_part.astype(jnp.float32), mps_part.astype(jnp.float32))
        pieces.append(product.astype(jnp.bfloat16))
    mixed_rows = jnp.stack(pieces, axis=1)

    def one_bond(running, inputs):
        mixed_bond, charge_bond, mpo_bond = inputs
        term_list = []
        zero_index = jnp.zeros((), jnp.int32)
        for phys_state in range(4):
            start_up = (2 - UP_CHARGE[phys_state] + charge_bond[0]).astype(jnp.int32)
            start_down = (2 - DOWN_CHARGE[phys_state] + charge_bond[1]).astype(jnp.int32)
            chosen = lax.dynamic_slice(proj_padded, (zero_index, start_up, start_down, zero_index, zero_index), (4, UP_VALUES, DOWN_VALUES, BLOCK_DIM, BLOCK_DIM))
            one_term = jnp.einsum('tudij,udik->tudjk', chosen.astype(jnp.float32), mixed_bond[phys_state].astype(jnp.float32))
            term_list.append(one_term.astype(jnp.bfloat16))
        projected = jnp.stack(term_list, axis=0).astype(jnp.float32)
        running = running + jnp.einsum('svt,stydjk->vydjk', mpo_bond.astype(jnp.float32), projected)
        return running, None

    start_sum = jnp.zeros((MPO_BOND, UP_VALUES, DOWN_VALUES, BLOCK_DIM, BLOCK_DIM), jnp.float32)
    running, unused = lax.scan(one_bond, start_sum, (mixed_rows, mpo_charge, mpo_masked))
    return running.astype(jnp.bfloat16)


def reference(env_in, mps, proj, mpo, mpo_charge, block_sizes):
    environment = env_in.reshape(MPO_BOND, UP_VALUES, DOWN_VALUES, BLOCK_DIM, BLOCK_DIM)
    outputs = []
    for site_index in range(CHAIN_SITES):
        mps_grid, proj_grid = mask_site(mps[site_index], proj[site_index], block_sizes[site_index], block_sizes[site_index + 1])
        proj_padded = jnp.pad(proj_grid, ((0, 0), (2, 2), (2, 2), (0, 0), (0, 0)))
        mpo_masked = mask_mpo(mpo[site_index], mpo_charge)
        environment = site_step(environment, mps_grid, proj_padded, mpo_masked, mpo_charge)
        outputs.append(environment.reshape(MPO_BOND, SECTORS, BLOCK_DIM, BLOCK_DIM))
    return jnp.stack(outputs, axis=0)
```

```python
import jax
import jax.numpy as jnp
from jax import lax
from jax.experimental import pallas as pl
from jax.experimental.pallas import tpu as pltpu
from jax.sharding import PartitionSpec as P

UP_VALUES = 8
DOWN_VALUES = 2
SECTORS = 16
BLOCK = 128
HALF = 64
MESH = pl.DeviceIdType.MESH

UP_CHARGE = (0, 1, 0, 1)
DOWN_CHARGE = (0, 0, 1, 1)
PHYS_ORDER = (0, 2, 1, 3)


def role_of(op):
    return op // 4, (op // 2) % 2, op % 2


def op_of(group, down, half):
    return group * 4 + down * 2 + half


def kernel(charge, coeff, env, mps_rows, proj_cols, out,
           slot, lbuf, mb, own, sib_s, sib_r, part_s, part_r, sbuf, obuf,
           slot_sem, next_ss, init_ss, sib_ss, sib_rs, part_ss, part_rs, out_ss, out_ls, out_rs):
    i = lax.axis_index("chain")
    op = lax.axis_index("op")
    g, d, k = role_of(op)
    me = d * 2 + k
    f32, bf16 = jnp.float32, jnp.bfloat16

    bar = pltpu.get_barrier_semaphore()

    def greet(chain, other):
        pl.semaphore_signal(bar, inc=1, device_id=(chain, other), device_id_type=MESH)

    @pl.when(i > 0)
    def _():
        for gg in range(4):
            greet(i - 1, op_of(gg, d, k))
        for mm in range(4):
            @pl.when(mm != me)
            def _():
                greet(i, op_of(g, mm // 2, mm % 2))

    @pl.when(i == 0)
    def _():
        for other in range(16):
            @pl.when(other != op)
            def _():
                greet(i, other)

    rows = lax.broadcasted_iota(jnp.int32, (1024, 64), 0)
    cols = lax.broadcasted_iota(jnp.int32, (1024, 64), 1)
    spread = jnp.where(rows // 16 == cols, 1.0, 0.0).astype(bf16)
    tall = jnp.dot(spread, coeff[...], preferred_element_type=f32).astype(bf16)
    rows = lax.broadcasted_iota(jnp.int32, (BLOCK, 256), 0)
    cols = lax.broadcasted_iota(jnp.int32, (BLOCK, 256), 1)
    widen = jnp.where(rows == cols // 16, 1.0, 0.0).astype(bf16)
    wide = jnp.dot(tall, widen, preferred_element_type=f32)
    rows = lax.broadcasted_iota(jnp.int32, (1024, 256), 0)
    cols = lax.broadcasted_iota(jnp.int32, (1024, 256), 1)
    mb[...] = jnp.where(rows % 16 == cols % 16, wide, 0.0).astype(bf16)
    lbuf[...] = jnp.zeros_like(lbuf)

    @pl.when(i == 0)
    def _():
        pl.semaphore_wait(bar, 19)

    @pl.when((i > 0) & (i < 7))
    def _():
        pl.semaphore_wait(bar, 7)

    @pl.when(i == 7)
    def _():
        pl.semaphore_wait(bar, 3)

    def init_row(u):
        mine = g * 4 + me
        for other in range(16):
            gg, dd, kk = role_of(other)

            @pl.when(other != op)
            def _():
                pltpu.make_async_remote_copy(
                    env.at[dd, kk, u], slot.at[u, :, mine], init_ss.at[u], slot_sem.at[u],
                    device_id=(i, other), device_id_type=MESH).start()

            @pl.when(other == op)
            def _():
                pltpu.make_async_copy(env.at[dd, kk, u], slot.at[u, :, mine], slot_sem.at[u]).start()

    @pl.when(i == 0)
    def _():
        def two(u, _):
            init_row(u)
            return 0
        lax.fori_loop(0, 2, two, 0)

    def mix(u, first, plane):
        for pair in range(2):
            x = slot[u, pair].reshape(256, 256)
            y = jnp.dot(mb[pl.ds((2 * first + plane) * 256, 256), :], x, preferred_element_type=f32).astype(bf16)
            for side in range(2):
                lbuf[plane, pl.ds((2 * pair + side) * 256, 256), pl.ds(first * BLOCK, BLOCK)] = (
                    y[:, side * BLOCK:(side + 1) * BLOCK])

    def apply(u, plane):
        grown = jnp.dot(lbuf[plane], mps_rows[u, plane], preferred_element_type=f32).astype(bf16)
        grown = grown.reshape(4, 4, HALF, BLOCK)
        for m in range(4):
            up = u + charge[g * 4 + m, 0]
            down = d + plane + charge[g * 4 + m, 1]
            inside = (up >= 0) & (up < UP_VALUES) & (down >= 0) & (down < DOWN_VALUES)
            place = jnp.where(inside, up * 2 + down, SECTORS)
            res = jnp.dot(proj_cols[place], grown[:, m].reshape(256, BLOCK), preferred_element_type=f32)
            own[plane, m] = res[:HALF]
            sib_s[u, plane, m] = res[HALF:].astype(bf16)

    def sibling(u, plane):
        return pltpu.make_async_remote_copy(
            sib_s.at[u, plane], sib_r.at[u, plane], sib_ss.at[u, plane], sib_rs.at[u, plane],
            device_id=(i, op_of(g, d, 1 - k)), device_id_type=MESH)

    def partial(u):
        return pltpu.make_async_remote_copy(
            part_s.at[u], part_r.at[u], part_ss.at[u], part_rs.at[u],
            device_id=(i, op_of(g, 1 - d, k)), device_id_type=MESH)

    def step(u, _):
        @pl.when((i == 0) & (u < 6))
        def _():
            init_row(u + 2)
        pltpu.make_async_copy(slot.at[u], slot.at[u], slot_sem.at[u]).wait()
        mix(u, 0, 0)
        apply(u, 0)
        sibling(u, 0).start()

        @pl.when(d == 0)
        def _():
            mix(u, 0, 1)
            apply(u, 1)
            sibling(u, 1).start()

        @pl.when(d == 1)
        def _():
            mix(u, 1, 0)
        sibling(u, 0).wait_recv()

        @pl.when(d == 1)
        def _():
            partial(u).wait_recv()
            for m in range(4):
                own[0, m] = own[0, m] + part_r[u, m].astype(f32)

        for m in range(4):
            res = (own[0, m] + sib_r[u, 0, m].astype(f32)).astype(bf16)
            obuf[u, m] = res
            for pair in range(2):
                for side in range(2):
                    start = pair * 32 + side * 16
                    sbuf[u, pair, m, :, pl.ds(side * BLOCK, BLOCK)] = res[start:start + 16]

        @pl.when(i < 7)
        def _():
            for gg in range(4):
                pltpu.make_async_remote_copy(
                    sbuf.at[u], slot.at[u, :, pl.ds(g * 4, 4)], next_ss.at[u], slot_sem.at[u],
                    device_id=(i + 1, op_of(gg, d, k)), device_id_type=MESH).start()

        @pl.when(d == 0)
        def _():
            sibling(u, 1).wait_recv()
            for m in range(4):
                part_s[u, m] = (own[1, m] + sib_r[u, 1, m].astype(f32)).astype(bf16)
            partial(u).start()

        for m in range(4):
            dst = out.at[u * 2 + d, pl.ds(k * HALF, HALF)]

            @pl.when(m != me)
            def _():
                pltpu.make_async_remote_copy(
                    obuf.at[u, m], dst, out_ss.at[u], out_rs,
                    device_id=(i, op_of(g, m // 2, m % 2)), device_id_type=MESH).start()

            @pl.when(m == me)
            def _():
                pltpu.make_async_copy(obuf.at[u, m], dst, out_ls.at[u]).start()

        @pl.when(d == 0)
        def _():
            mix(u, 1, 0)
            mix(u, 1, 1)
        return 0

    lax.fori_loop(0, UP_VALUES, step, 0)

    def drain(u, _):
        @pl.when(i == 0)
        def _():
            part = slot.at[u, :, pl.ds(0, 15)]
            pltpu.make_async_copy(part, part, init_ss.at[u]).wait()

        @pl.when(i < 7)
        def _():
            pltpu.make_async_copy(slot.at[u], slot.at[u], next_ss.at[u]).wait()
        sibling(u, 0).wait_send()

        @pl.when(d == 0)
        def _():
            sibling(u, 1).wait_send()
            partial(u).wait_send()
        three = obuf.at[u, pl.ds(0, 3)]
        pltpu.make_async_copy(three, three, out_ss.at[u]).wait()
        pltpu.make_async_copy(obuf.at[u, 0], obuf.at[u, 0], out_ls.at[u]).wait()
        return 0

    lax.fori_loop(0, UP_VALUES, drain, 0)
    pltpu.make_async_copy(out.at[pl.ds(0, 12)], out.at[pl.ds(0, 12)], out_rs).wait()


def mask_mpo(site_mpo, mpo_charge):
    up_state = jnp.array(UP_CHARGE, dtype=jnp.int32)
    down_state = jnp.array(DOWN_CHARGE, dtype=jnp.int32)
    up_bond = mpo_charge[:, 0]
    down_bond = mpo_charge[:, 1]
    match_up = (
        up_bond[:, None, None, None] + up_state[None, None, None, :]
        == up_state[None, :, None, None] + up_bond[None, None, :, None]
    )
    match_down = (
        down_bond[:, None, None, None] + down_state[None, None, None, :]
        == down_state[None, :, None, None] + down_bond[None, None, :, None]
    )
    return jnp.where(match_up & match_down, site_mpo, jnp.zeros_like(site_mpo))


def on_device(env_in, mps, proj, mpo, mpo_charge, block_sizes):
    i = lax.axis_index("chain")
    g, d, k = role_of(lax.axis_index("op"))
    bf16 = jnp.bfloat16

    masked = mask_mpo(mpo[0], mpo_charge)
    charge = mpo_charge
    mine = lax.dynamic_slice_in_dim(masked, g * 4, 4, 2)
    coeff = jnp.stack([mine[:, p] for p in PHYS_ORDER], axis=0).transpose(0, 2, 3, 1).reshape(64, 16)
    coeff = jnp.pad(coeff, ((0, 0), (0, BLOCK - 16)))

    left = lax.dynamic_index_in_dim(block_sizes, i, 0, keepdims=False).reshape(UP_VALUES, DOWN_VALUES)
    right = lax.dynamic_index_in_dim(block_sizes, i + 1, 0, keepdims=False).reshape(UP_VALUES, DOWN_VALUES)
    right = jnp.pad(right, ((0, 1), (0, 1)))
    left = lax.dynamic_index_in_dim(left, d, 1, keepdims=False)
    right_same = lax.dynamic_index_in_dim(right, d, 1, keepdims=False)
    right_more = lax.dynamic_index_in_dim(right, d + 1, 1, keepdims=False)
    grid = lax.dynamic_index_in_dim(mps[0].reshape(4, UP_VALUES, DOWN_VALUES, BLOCK, BLOCK), d, 2, keepdims=False)
    pos = jnp.arange(BLOCK, dtype=jnp.int32)
    planes = []
    for p in range(4):
        r = right_more if DOWN_CHARGE[p] else right_same
        r = r[UP_CHARGE[p]:UP_CHARGE[p] + UP_VALUES]
        keep = (pos[None, :, None] < left[:, None, None]) & (pos[None, None, :] < r[:, None, None])
        block = jnp.where(keep, grid[p], jnp.zeros_like(grid[p]))
        if UP_CHARGE[p]:
            block = jnp.pad(block[:-1], ((1, 0), (0, 0), (0, 0)))
        planes.append(block)
    mps_rows = jnp.stack(planes, axis=1).reshape(UP_VALUES, 2, 256, BLOCK)

    pgrid = lax.dynamic_slice_in_dim(proj[0].reshape(4, UP_VALUES, DOWN_VALUES, BLOCK, BLOCK), k * HALF, HALF, 3)
    parts = []
    for t in range(4):
        up, down = UP_CHARGE[t], DOWN_CHARGE[t]
        part = pgrid[t][:UP_VALUES - up, :DOWN_VALUES - down]
        parts.append(jnp.pad(part, ((up, 0), (down, 0), (0, 0), (0, 0))))
    stacked = jnp.stack(parts, axis=2).reshape(SECTORS, 4, 4, 16, 2, HALF)
    stacked = jnp.where(k == 0, stacked, stacked[:, :, :, :, ::-1])
    proj_cols = stacked.transpose(0, 4, 5, 2, 1, 3).reshape(SECTORS, BLOCK, 256)
    proj_cols = jnp.pad(proj_cols, ((0, 1), (0, 0), (0, 0)))

    env = env_in[0].reshape(UP_VALUES, 2, 2, 2, 2, 16, BLOCK).transpose(1, 2, 0, 3, 5, 4, 6)
    env = env.reshape(2, 2, UP_VALUES, 2, 16, 256)

    vm = pl.BlockSpec(memory_space=pltpu.VMEM)
    dma = pltpu.SemaphoreType.DMA
    out = pl.pallas_call(
        kernel,
        out_shape=jax.ShapeDtypeStruct((SECTORS, BLOCK, BLOCK), bf16),
        in_specs=[pl.BlockSpec(memory_space=pltpu.SMEM), vm, vm, vm, vm],
        out_specs=pl.BlockSpec(memory_space=pl.ANY),
        scratch_shapes=[
            pltpu.VMEM((UP_VALUES, 2, 16, 16, 256), bf16),
            pltpu.VMEM((2, 1024, 256), bf16),
            pltpu.VMEM((1024, 256), bf16),
            pltpu.VMEM((2, 4, HALF, BLOCK), jnp.float32),
            pltpu.VMEM((UP_VALUES, 2, 4, HALF, BLOCK), bf16),
            pltpu.VMEM((UP_VALUES, 2, 4, HALF, BLOCK), bf16),
            pltpu.VMEM((UP_VALUES, 4, HALF, BLOCK), bf16),
            pltpu.VMEM((UP_VALUES, 4, HALF, BLOCK), bf16),
            pltpu.VMEM((UP_VALUES, 2, 4, 16, 256), bf16),
            pltpu.VMEM((UP_VALUES, 4, HALF, BLOCK), bf16),
            dma((8,)), dma((8,)), dma((8,)), dma((8, 2)), dma((8, 2)), dma((8,)), dma((8,)), dma((8,)), dma((8,)), dma,
        ],
        compiler_params=pltpu.CompilerParams(collective_id=0, has_side_effects=True, vmem_limit_bytes=40 << 20),
        name="sweep",
    )(charge, coeff, env, mps_rows, proj_cols)
    return out[None, None]


def solution(mesh):
    return jax.shard_map(
        on_device,
        mesh=mesh,
        in_specs=(
            P("op", None, None, None),
            P("chain", None, None, None, None),
            P("chain", None, None, None, None),
            P("chain", None, None, None, None),
            P(),
            P(),
        ),
        out_specs=P("chain", "op", None, None, None),
        check_vma=False,
    )
```

```python
import jax
import jax.numpy as jnp
from jax import lax
from jax.experimental import pallas as pl
from jax.experimental.pallas import tpu as pltpu
from jax.sharding import PartitionSpec as P

UP_VALUES = 8
DOWN_VALUES = 2
SECTORS = 16
BLOCK = 128
HALF = 64
AHEAD = 3
MESH = pl.DeviceIdType.MESH

UP_CHARGE = (0, 1, 0, 1)
DOWN_CHARGE = (0, 0, 1, 1)
PHYS_ORDER = (0, 2, 1, 3)


def role_of(op):
    y = op // 4
    return (op // 2) % 2 * 2 + y % 2, y // 2, op % 2


def op_of(group, down, half):
    return (down * 2 + group % 2) * 4 + group // 2 * 2 + half


def bond_of(group, member):
    return op_of(group, member // 2, member % 2)


def kernel(charge, sizes, coeff, env, mps, proj, out,
           slot, lbuf, mb, own, sib_s, sib_r, part_s, part_r, sbuf, obuf, env_r, mrows, pcols,
           slot_sem, next_ss, init_ss, sib_ss, sib_rs, part_ss, part_rs, out_ss, out_ls, load_sem, out_rs):
    i = lax.axis_index("chain")
    op = lax.axis_index("op")
    g, d, k = role_of(op)
    me = d * 2 + k
    f32, bf16 = jnp.float32, jnp.bfloat16

    bar = pltpu.get_barrier_semaphore()

    def greet(chain, group, down, half):
        pl.semaphore_signal(bar, inc=1, device_id=(chain, op_of(group, down, half)), device_id_type=MESH)

    @pl.when(i > 0)
    def _():
        for j in range(4):
            greet(i - 1, (g + j) % 4, d, k)

    @pl.when(i == 0)
    def _():
        for j in range(8):
            greet(1, (g + j // 2) % 4, 1 - d, (k + j) % 2)
        for j in range(2, 8):
            greet(0, (g + j // 2) % 4, d, (k + j) % 2)
    greet(i, g, d, 1 - k)
    greet(i, g, 1 - d, k)
    greet(i, g, 1 - d, 1 - k)

    target_down = (d + i) % 2

    def env_load(half, side):
        return pltpu.make_async_copy(
            env.at[:, target_down, half, :, side], env_r.at[half, :, :, :, pl.ds(side * BLOCK, BLOCK)], load_sem.at[0])

    @pl.when(i < 2)
    def _():
        for half in range(2):
            for side in range(2):
                env_load(half, side).start()

    def mps_load(p):
        up = UP_CHARGE[p]
        return pltpu.make_async_copy(
            mps.at[p, pl.ds(0, UP_VALUES - up), d], mrows.at[pl.ds(up, UP_VALUES - up), p // 2, up], load_sem.at[1 + p])

    def proj_load(t):
        up, down = UP_CHARGE[t], DOWN_CHARGE[t]
        return pltpu.make_async_copy(
            proj.at[t, pl.ds(0, UP_VALUES - up), pl.ds(0, DOWN_VALUES - down), pl.ds(k * HALF, HALF)],
            pcols.at[pl.ds(up, UP_VALUES - up), pl.ds(down, DOWN_VALUES - down), t], load_sem.at[5 + t])
    for p in range(4):
        mps_load(p).start()
        proj_load(p).start()
    zero = jnp.zeros((HALF, BLOCK), bf16)
    for t in range(4):
        pcols[UP_VALUES, 0, t] = zero
        for down in range(2):
            if UP_CHARGE[t]:
                pcols[0, down, t] = zero
        if DOWN_CHARGE[t]:
            for up in range(UP_CHARGE[t], UP_VALUES):
                pcols[up, 0, t] = zero
    for plane in range(2):
        mrows[0, plane, 1] = jnp.zeros((BLOCK, BLOCK), bf16)
    lbuf[...] = jnp.zeros_like(lbuf)

    rows = lax.broadcasted_iota(jnp.int32, (16, 64), 0)
    cols = lax.broadcasted_iota(jnp.int32, (16, 64), 1)
    pick = jnp.where(cols == bond_of(g, rows // 4) * 4 + rows % 4, 1.0, 0.0).astype(bf16)
    mine = lax.dot_general(pick, coeff[...], (((1,), (1,)), ((), ())), preferred_element_type=f32).astype(bf16)
    rows = lax.broadcasted_iota(jnp.int32, (16, 256), 0)
    cols = lax.broadcasted_iota(jnp.int32, (16, 256), 1)
    col_up = jnp.zeros((16, 256), jnp.int32)
    col_down = jnp.zeros((16, 256), jnp.int32)
    row_up = -(rows % 2)
    row_down = -((rows // 2) % 2)
    for n in range(16):
        b = bond_of(n // 4, n % 4)
        col_up = jnp.where(cols // 16 == n, charge[b, 0], col_up)
        col_down = jnp.where(cols // 16 == n, charge[b, 1], col_down)
    for m in range(4):
        b = bond_of(g, m)
        row_up = row_up + jnp.where(rows // 4 == m, charge[b, 0], 0)
        row_down = row_down + jnp.where(rows // 4 == m, charge[b, 1], 0)
    rows = lax.broadcasted_iota(jnp.int32, (64, 256), 0)
    cols = lax.broadcasted_iota(jnp.int32, (64, 256), 1)
    slot_bond = bond_of(cols // 64, cols // 16 % 4)
    long_rows = lax.broadcasted_iota(jnp.int32, (256, 256), 0)
    long_cols = lax.broadcasted_iota(jnp.int32, (256, 256), 1)
    repeat = jnp.where(
        lax.broadcasted_iota(jnp.int32, (256, 16), 0) // 16 == lax.broadcasted_iota(jnp.int32, (256, 16), 1),
        1.0, 0.0).astype(bf16)
    for place, p in enumerate(PHYS_ORDER):
        widen = jnp.where(rows == slot_bond * 4 + p, 1.0, 0.0).astype(bf16)
        wide = jnp.dot(mine, widen, preferred_element_type=f32)
        match = (col_up == row_up + UP_CHARGE[p]) & (col_down == row_down + DOWN_CHARGE[p])
        wide = jnp.where(match, wide, 0.0).astype(bf16)
        tall = jnp.dot(repeat, wide, preferred_element_type=f32)
        mb[place * 256:(place + 1) * 256, :] = jnp.where(long_rows % 16 == long_cols % 16, tall, 0.0).astype(bf16)

    @pl.when(i == 0)
    def _():
        pl.semaphore_wait(bar, 13)

    @pl.when(i == 1)
    def _():
        pl.semaphore_wait(bar, 15)

    @pl.when((i > 1) & (i < 7))
    def _():
        pl.semaphore_wait(bar, 7)

    @pl.when(i == 7)
    def _():
        pl.semaphore_wait(bar, 3)

    place = g * 4 + me

    def init_row(u, first):
        for j in range(first, 8):
            half = (k + j) % 2
            pltpu.make_async_remote_copy(
                env_r.at[half, u], slot.at[u, :, place], init_ss.at[u], slot_sem.at[u],
                device_id=(0, op_of((g + j // 2) % 4, target_down, half)), device_id_type=MESH).start()

    def init_own(u):
        init_row(u, 1)
        pltpu.make_async_copy(env_r.at[k, u], slot.at[u, :, place], slot_sem.at[u]).start()

    @pl.when(i < 2)
    def _():
        pltpu.make_async_copy(env_r, env_r, load_sem.at[0]).wait()

    @pl.when(i == 0)
    def _():
        def start(u, _):
            init_own(u)
            return 0
        lax.fori_loop(0, AHEAD, start, 0)

    @pl.when(i == 1)
    def _():
        def start(u, _):
            init_row(u, 0)
            return 0
        lax.fori_loop(0, UP_VALUES, start, 0)

    for p in range(4):
        mps_load(p).wait()
    rows = lax.broadcasted_iota(jnp.int32, (BLOCK, BLOCK), 0)
    cols = lax.broadcasted_iota(jnp.int32, (BLOCK, BLOCK), 1)

    def mask_row(u, _):
        for plane in range(2):
            for up in range(2):
                left = sizes[i, jnp.maximum(u - up, 0) * 2 + d]
                right = sizes[i + 1, u * 2 + jnp.minimum(d + plane, 1)]
                keep = (rows < left) & (cols < right)
                mrows[u, plane, up] = jnp.where(keep, mrows[u, plane, up].astype(f32), 0.0).astype(bf16)
        return 0
    lax.fori_loop(0, UP_VALUES, mask_row, 0)
    for t in range(4):
        proj_load(t).wait()

    def mix(u, first, planes):
        for pair in range(2):
            x = slot[u, pair].reshape(256, 256)
            y = jnp.dot(mb[first * 512:first * 512 + planes * 256, :], x, preferred_element_type=f32).astype(bf16)
            for side in range(2):
                for plane in range(planes):
                    lbuf[plane, pl.ds((2 * pair + side) * 256, 256), pl.ds(first * BLOCK, BLOCK)] = (
                        y[plane * 256:(plane + 1) * 256, side * BLOCK:(side + 1) * BLOCK])

    def apply(u, plane):
        grown = jnp.dot(lbuf[plane], mrows[u, plane].reshape(256, BLOCK), preferred_element_type=f32).astype(bf16)
        for m in range(4):
            b = bond_of(g, m)
            up = u + charge[b, 0]
            down = d + plane + charge[b, 1]
            inside = (up >= 0) & (up < UP_VALUES) & (down >= 0) & (down < DOWN_VALUES)
            up = jnp.where(inside, up, UP_VALUES)
            down = jnp.where(inside, down, 0)
            piece = jnp.concatenate(
                [grown[at * 256 + m * 64 + t * 16:at * 256 + m * 64 + t * 16 + 16] for t in range(4) for at in range(4)], axis=0)
            res = lax.dot_general(pcols[up, down].reshape(256, BLOCK), piece, (((0,), (0,)), ((), ())),
                                  preferred_element_type=f32)
            own[plane, m] = jnp.where(k == 0, res[:HALF], res[HALF:])
            sib_s[u, plane, m] = jnp.where(k == 0, res[HALF:], res[:HALF]).astype(bf16)

    def sibling(u, plane):
        return pltpu.make_async_remote_copy(
            sib_s.at[u, plane], sib_r.at[u, plane], sib_ss.at[u, plane], sib_rs.at[u, plane],
            device_id=(i, op_of(g, d, 1 - k)), device_id_type=MESH)

    def partial(u):
        return pltpu.make_async_remote_copy(
            part_s.at[u], part_r.at[u], part_ss.at[u], part_rs.at[u],
            device_id=(i, op_of(g, 1 - d, k)), device_id_type=MESH)

    def step(u, _):
        @pl.when((i == 0) & (u < UP_VALUES - AHEAD))
        def _():
            init_own(u + AHEAD)
        pltpu.make_async_copy(slot.at[u], slot.at[u], slot_sem.at[u]).wait()

        @pl.when(d == 0)
        def _():
            mix(u, 0, 2)

        @pl.when(d == 1)
        def _():
            mix(u, 0, 1)
        apply(u, 0)
        sibling(u, 0).start()

        @pl.when(d == 0)
        def _():
            apply(u, 1)
            sibling(u, 1).start()

        @pl.when(d == 1)
        def _():
            mix(u, 1, 1)
        sibling(u, 0).wait_recv()

        @pl.when(d == 1)
        def _():
            partial(u).wait_recv()
            for m in range(4):
                own[0, m] = own[0, m] + part_r[u, m].astype(f32)

        for m in range(4):
            res = (own[0, m] + sib_r[u, 0, m].astype(f32)).astype(bf16)
            obuf[u, m] = res
            for pair in range(2):
                for side in range(2):
                    start = pair * 32 + side * 16
                    sbuf[u, pair, m, :, pl.ds(side * BLOCK, BLOCK)] = res[start:start + 16]

        @pl.when(i < 7)
        def _():
            for j in range(4):
                pltpu.make_async_remote_copy(
                    sbuf.at[u], slot.at[u, :, pl.ds(g * 4, 4)], next_ss.at[u], slot_sem.at[u],
                    device_id=(i + 1, op_of((g + j) % 4, d, k)), device_id_type=MESH).start()

        @pl.when(d == 0)
        def _():
            sibling(u, 1).wait_recv()
            for m in range(4):
                part_s[u, m] = (own[1, m] + sib_r[u, 1, m].astype(f32)).astype(bf16)
            partial(u).start()

        dst = out.at[u * 2 + d, pl.ds(k * HALF, HALF)]
        for j in range(1, 4):
            m = (me + j) % 4
            pltpu.make_async_remote_copy(
                obuf.at[u, m], dst, out_ss.at[u], out_rs,
                device_id=(i, bond_of(g, m)), device_id_type=MESH).start()
        pltpu.make_async_copy(obuf.at[u, me], dst, out_ls.at[u]).start()

        @pl.when(d == 0)
        def _():
            mix(u, 1, 2)
        return 0

    lax.fori_loop(0, UP_VALUES, step, 0)

    def drain(u, _):
        @pl.when(i == 0)
        def _():
            part = slot.at[u, :, pl.ds(0, 7)]
            pltpu.make_async_copy(part, part, init_ss.at[u]).wait()

        @pl.when(i == 1)
        def _():
            part = slot.at[u, :, pl.ds(0, 8)]
            pltpu.make_async_copy(part, part, init_ss.at[u]).wait()

        @pl.when(i < 7)
        def _():
            pltpu.make_async_copy(slot.at[u], slot.at[u], next_ss.at[u]).wait()
        sibling(u, 0).wait_send()

        @pl.when(d == 0)
        def _():
            sibling(u, 1).wait_send()
            partial(u).wait_send()
        three = obuf.at[u, pl.ds(0, 3)]
        pltpu.make_async_copy(three, three, out_ss.at[u]).wait()
        pltpu.make_async_copy(obuf.at[u, 0], obuf.at[u, 0], out_ls.at[u]).wait()
        return 0

    lax.fori_loop(0, UP_VALUES, drain, 0)
    pltpu.make_async_copy(out.at[pl.ds(0, 12)], out.at[pl.ds(0, 12)], out_rs).wait()


def on_device(env_in, mps, proj, mpo, mpo_charge, block_sizes):
    bf16 = jnp.bfloat16
    vm = pl.BlockSpec(memory_space=pltpu.VMEM)
    sm = pl.BlockSpec(memory_space=pltpu.SMEM)
    hbm = pl.BlockSpec(memory_space=pl.ANY)
    dma = pltpu.SemaphoreType.DMA
    out = pl.pallas_call(
        kernel,
        out_shape=jax.ShapeDtypeStruct((SECTORS, BLOCK, BLOCK), bf16),
        in_specs=[sm, sm, vm, hbm, hbm, hbm],
        out_specs=hbm,
        scratch_shapes=[
            pltpu.VMEM((UP_VALUES, 2, 16, 16, 256), bf16),
            pltpu.VMEM((2, 1024, 256), bf16),
            pltpu.VMEM((1024, 256), bf16),
            pltpu.VMEM((2, 4, HALF, BLOCK), jnp.float32),
            pltpu.VMEM((UP_VALUES, 2, 4, HALF, BLOCK), bf16),
            pltpu.VMEM((UP_VALUES, 2, 4, HALF, BLOCK), bf16),
            pltpu.VMEM((UP_VALUES, 4, HALF, BLOCK), bf16),
            pltpu.VMEM((UP_VALUES, 4, HALF, BLOCK), bf16),
            pltpu.VMEM((UP_VALUES, 2, 4, 16, 256), bf16),
            pltpu.VMEM((UP_VALUES, 4, HALF, BLOCK), bf16),
            pltpu.VMEM((2, UP_VALUES, 2, 16, 256), bf16),
            pltpu.VMEM((UP_VALUES, 2, 2, BLOCK, BLOCK), bf16),
            pltpu.VMEM((UP_VALUES + 1, 2, 4, HALF, BLOCK), bf16),
            dma((8,)), dma((8,)), dma((8,)), dma((8, 2)), dma((8, 2)), dma((8,)), dma((8,)), dma((8,)), dma((8,)),
            dma((9,)), dma,
        ],
        compiler_params=pltpu.CompilerParams(collective_id=0, has_side_effects=True, vmem_limit_bytes=40 << 20),
        name="sweep",
    )(
        mpo_charge, block_sizes, mpo.reshape(64, 64),
        env_in.reshape(UP_VALUES, 2, 2, 2, 2, 16, BLOCK),
        mps.reshape(4, UP_VALUES, DOWN_VALUES, BLOCK, BLOCK),
        proj.reshape(4, UP_VALUES, DOWN_VALUES, BLOCK, BLOCK),
    )
    return out[None, None]


def solution(mesh):
    return jax.shard_map(
        on_device,
        mesh=mesh,
        in_specs=(
            P("op", None, None, None),
            P("chain", None, None, None, None),
            P("chain", None, None, None, None),
            P("chain", None, None, None, None),
            P(),
            P(),
        ),
        out_specs=P("chain", "op", None, None, None),
        check_vma=False,
    )
```

```python
import jax
import jax.numpy as jnp
from jax import lax
from jax.experimental import pallas as pl
from jax.experimental.pallas import tpu as pltpu
from jax.sharding import PartitionSpec as P

UP_VALUES = 8
DOWN_VALUES = 2
SECTORS = 16
BLOCK = 128
HALF = 64
MESH = pl.DeviceIdType.MESH

UP_CHARGE = (0, 1, 0, 1)
DOWN_CHARGE = (0, 0, 1, 1)
PHYS_ORDER = (0, 2, 1, 3)
INIT_ROUTES = ((0, 0, (0, 1)), (1, 1, (0, 3)), (2, 0, (2, 3)), (7, 1, (1, 2)))


def role_of(op):
    y = op // 4
    return (op // 2) % 2 * 2 + y % 2, y // 2, op % 2


def op_of(group, down, half):
    return (down * 2 + group % 2) * 4 + group // 2 * 2 + half


def bond_of(group, member):
    return op_of(group, member // 2, member % 2)


def kernel(charge, sizes, coeff, env, mps, proj, out,
           slot, lbuf, mb, own, sib_s, sib_r, part_s, part_r, sbuf, obuf, env_r, mrows, pcols,
           slot_sem, next_ss, init_ss, sib_ss, sib_rs, part_ss, part_rs, out_ss, out_ls, load_sem, out_rs):
    i = lax.axis_index("chain")
    op = lax.axis_index("op")
    g, d, k = role_of(op)
    me = d * 2 + k
    f32, bf16 = jnp.float32, jnp.bfloat16

    bar = pltpu.get_barrier_semaphore()

    def near(step, flip, half):
        z = (op // 2) % 2
        z = 1 - z if flip else z
        return (op // 4 + step) % 4 * 4 + z * 2 + half

    def greet(chain, group, down, half):
        pl.semaphore_signal(bar, inc=1, device_id=(chain, op_of(group, down, half)), device_id_type=MESH)

    @pl.when(i > 0)
    def _():
        for j in range(4):
            greet(i - 1, (g + j) % 4, d, k)

    @pl.when(i == 0)
    def _():
        for source, flip, steps in INIT_ROUTES:
            for step in steps:
                for half in range(2):
                    if source or step:
                        pl.semaphore_signal(
                            bar, inc=1, device_id=(source, near(4 - step, flip, half)), device_id_type=MESH)
    greet(i, g, d, 1 - k)
    greet(i, g, 1 - d, k)
    greet(i, g, 1 - d, 1 - k)

    spreads = (i < 3) | (i == 7)

    @pl.when(spreads)
    def _():
        for down in range(2):
            for half in range(2):
                for side in range(2):
                    pltpu.make_async_copy(
                        env.at[:, down, half, :, side], env_r.at[down, half, :, :, :, pl.ds(side * BLOCK, BLOCK)],
                        load_sem.at[0]).start()

    def mps_load(p):
        up = UP_CHARGE[p]
        return pltpu.make_async_copy(
            mps.at[p, pl.ds(0, UP_VALUES - up), d], mrows.at[pl.ds(up, UP_VALUES - up), p // 2, up], load_sem.at[1 + p])

    def proj_load(t):
        up, down = UP_CHARGE[t], DOWN_CHARGE[t]
        return pltpu.make_async_copy(
            proj.at[t, pl.ds(0, UP_VALUES - up), pl.ds(0, DOWN_VALUES - down), pl.ds(k * HALF, HALF)],
            pcols.at[pl.ds(up, UP_VALUES - up), pl.ds(down, DOWN_VALUES - down), t], load_sem.at[5 + t])
    for p in range(4):
        mps_load(p).start()
        proj_load(p).start()
    zero = jnp.zeros((HALF, BLOCK), bf16)
    for t in range(4):
        pcols[UP_VALUES, 0, t] = zero
        for down in range(2):
            if UP_CHARGE[t]:
                pcols[0, down, t] = zero
        if DOWN_CHARGE[t]:
            for up in range(UP_CHARGE[t], UP_VALUES):
                pcols[up, 0, t] = zero
    for plane in range(2):
        mrows[0, plane, 1] = jnp.zeros((BLOCK, BLOCK), bf16)
    lbuf[...] = jnp.zeros_like(lbuf)

    rows = lax.broadcasted_iota(jnp.int32, (16, 64), 0)
    cols = lax.broadcasted_iota(jnp.int32, (16, 64), 1)
    pick = jnp.where(cols == bond_of(g, rows // 4) * 4 + rows % 4, 1.0, 0.0).astype(bf16)
    mine = lax.dot_general(pick, coeff[...], (((1,), (1,)), ((), ())), preferred_element_type=f32).astype(bf16)
    rows = lax.broadcasted_iota(jnp.int32, (16, 256), 0)
    cols = lax.broadcasted_iota(jnp.int32, (16, 256), 1)
    col_up = jnp.zeros((16, 256), jnp.int32)
    col_down = jnp.zeros((16, 256), jnp.int32)
    row_up = -(rows % 2)
    row_down = -((rows // 2) % 2)
    for n in range(16):
        b = bond_of(n // 4, n % 4)
        col_up = jnp.where(cols // 16 == n, charge[b, 0], col_up)
        col_down = jnp.where(cols // 16 == n, charge[b, 1], col_down)
    for m in range(4):
        b = bond_of(g, m)
        row_up = row_up + jnp.where(rows // 4 == m, charge[b, 0], 0)
        row_down = row_down + jnp.where(rows // 4 == m, charge[b, 1], 0)
    rows = lax.broadcasted_iota(jnp.int32, (64, 256), 0)
    cols = lax.broadcasted_iota(jnp.int32, (64, 256), 1)
    slot_bond = bond_of(cols // 64, cols // 16 % 4)
    long_rows = lax.broadcasted_iota(jnp.int32, (256, 256), 0)
    long_cols = lax.broadcasted_iota(jnp.int32, (256, 256), 1)
    repeat = jnp.where(
        lax.broadcasted_iota(jnp.int32, (256, 16), 0) // 16 == lax.broadcasted_iota(jnp.int32, (256, 16), 1),
        1.0, 0.0).astype(bf16)
    for place, p in enumerate(PHYS_ORDER):
        widen = jnp.where(rows == slot_bond * 4 + p, 1.0, 0.0).astype(bf16)
        wide = jnp.dot(mine, widen, preferred_element_type=f32)
        match = (col_up == row_up + UP_CHARGE[p]) & (col_down == row_down + DOWN_CHARGE[p])
        wide = jnp.where(match, wide, 0.0).astype(bf16)
        tall = jnp.dot(repeat, wide, preferred_element_type=f32)
        mb[place * 256:(place + 1) * 256, :] = jnp.where(long_rows % 16 == long_cols % 16, tall, 0.0).astype(bf16)

    @pl.when(i == 0)
    def _():
        pl.semaphore_wait(bar, 9)

    @pl.when((i == 1) | (i == 2))
    def _():
        pl.semaphore_wait(bar, 11)

    @pl.when(i > 2)
    def _():
        pl.semaphore_wait(bar, 7)

    place = g * 4 + me

    @pl.when(spreads)
    def _():
        pltpu.make_async_copy(env_r, env_r, load_sem.at[0]).wait()

    for source, flip, steps in INIT_ROUTES:
        def init_row(u, _):
            for step in steps:
                down = (op // 4 + step) % 4 // 2
                for half in range(2):
                    copy = pltpu.make_async_remote_copy(
                        env_r.at[down, half, u], slot.at[u, :, place], init_ss.at[u], slot_sem.at[u],
                        device_id=(0, near(step, flip, half)), device_id_type=MESH)
                    if source or step:
                        copy.start()
                    else:
                        @pl.when(half != k)
                        def _():
                            copy.start()
            if source == 0:
                pltpu.make_async_copy(env_r.at[d, k, u], slot.at[u, :, place], slot_sem.at[u]).start()
            return 0

        @pl.when(i == source)
        def _():
            lax.fori_loop(0, UP_VALUES, init_row, 0)

    for p in range(4):
        mps_load(p).wait()
    rows = lax.broadcasted_iota(jnp.int32, (BLOCK, BLOCK), 0)
    cols = lax.broadcasted_iota(jnp.int32, (BLOCK, BLOCK), 1)

    def mask_row(u, _):
        for plane in range(2):
            for up in range(2):
                left = sizes[i, jnp.maximum(u - up, 0) * 2 + d]
                right = sizes[i + 1, u * 2 + jnp.minimum(d + plane, 1)]
                keep = (rows < left) & (cols < right)
                mrows[u, plane, up] = jnp.where(keep, mrows[u, plane, up].astype(f32), 0.0).astype(bf16)
        return 0
    lax.fori_loop(0, UP_VALUES, mask_row, 0)
    for t in range(4):
        proj_load(t).wait()

    def mix(u, first, planes):
        for pair in range(2):
            x = slot[u, pair].reshape(256, 256)
            y = jnp.dot(mb[first * 512:first * 512 + planes * 256, :], x, preferred_element_type=f32).astype(bf16)
            for side in range(2):
                for plane in range(planes):
                    lbuf[plane, pl.ds((2 * pair + side) * 256, 256), pl.ds(first * BLOCK, BLOCK)] = (
                        y[plane * 256:(plane + 1) * 256, side * BLOCK:(side + 1) * BLOCK])

    def apply(u, plane):
        grown = jnp.dot(lbuf[plane], mrows[u, plane].reshape(256, BLOCK), preferred_element_type=f32).astype(bf16)
        for m in range(4):
            b = bond_of(g, m)
            up = u + charge[b, 0]
            down = d + plane + charge[b, 1]
            inside = (up >= 0) & (up < UP_VALUES) & (down >= 0) & (down < DOWN_VALUES)
            up = jnp.where(inside, up, UP_VALUES)
            down = jnp.where(inside, down, 0)
            piece = jnp.concatenate(
                [grown[at * 256 + m * 64 + t * 16:at * 256 + m * 64 + t * 16 + 16] for t in range(4) for at in range(4)], axis=0)
            res = lax.dot_general(pcols[up, down].reshape(256, BLOCK), piece, (((0,), (0,)), ((), ())),
                                  preferred_element_type=f32)
            own[plane, m] = jnp.where(k == 0, res[:HALF], res[HALF:])
            sib_s[u, plane, m] = jnp.where(k == 0, res[HALF:], res[:HALF]).astype(bf16)

    def sibling(u, plane):
        return pltpu.make_async_remote_copy(
            sib_s.at[u, plane], sib_r.at[u, plane], sib_ss.at[u, plane], sib_rs.at[u, plane],
            device_id=(i, op_of(g, d, 1 - k)), device_id_type=MESH)

    def partial(u):
        return pltpu.make_async_remote_copy(
            part_s.at[u], part_r.at[u], part_ss.at[u], part_rs.at[u],
            device_id=(i, op_of(g, 1 - d, k)), device_id_type=MESH)

    def give(u, _):
        dst = out.at[u * 2 + d, pl.ds(k * HALF, HALF)]
        for j in range(1, 4):
            m = (me + j) % 4
            pltpu.make_async_remote_copy(
                obuf.at[u, m], dst, out_ss.at[u], out_rs,
                device_id=(i, bond_of(g, m)), device_id_type=MESH).start()
        pltpu.make_async_copy(obuf.at[u, me], dst, out_ls.at[u]).start()
        return 0

    def step(u, _):
        pltpu.make_async_copy(slot.at[u], slot.at[u], slot_sem.at[u]).wait()

        @pl.when(d == 0)
        def _():
            mix(u, 0, 2)

        @pl.when(d == 1)
        def _():
            mix(u, 0, 1)
        apply(u, 0)
        sibling(u, 0).start()

        @pl.when(d == 0)
        def _():
            apply(u, 1)
            sibling(u, 1).start()
            mix(u, 1, 2)

        @pl.when(d == 1)
        def _():
            mix(u, 1, 1)
        sibling(u, 0).wait_recv()

        @pl.when(d == 1)
        def _():
            partial(u).wait_recv()
            for m in range(4):
                own[0, m] = own[0, m] + part_r[u, m].astype(f32)

        for m in range(4):
            res = (own[0, m] + sib_r[u, 0, m].astype(f32)).astype(bf16)
            obuf[u, m] = res
            for pair in range(2):
                for side in range(2):
                    start = pair * 32 + side * 16
                    sbuf[u, pair, m, :, pl.ds(side * BLOCK, BLOCK)] = res[start:start + 16]

        @pl.when(i < 7)
        def _():
            for j in range(4):
                pltpu.make_async_remote_copy(
                    sbuf.at[u], slot.at[u, :, pl.ds(g * 4, 4)], next_ss.at[u], slot_sem.at[u],
                    device_id=(i + 1, op_of((g + j) % 4, d, k)), device_id_type=MESH).start()

        @pl.when(d == 0)
        def _():
            sibling(u, 1).wait_recv()
            for m in range(4):
                part_s[u, m] = (own[1, m] + sib_r[u, 1, m].astype(f32)).astype(bf16)
            partial(u).start()

        @pl.when(i == 7)
        def _():
            give(u, 0)
        return 0

    lax.fori_loop(0, UP_VALUES, step, 0)

    @pl.when(i < 7)
    def _():
        lax.fori_loop(0, UP_VALUES, give, 0)

    def drain(u, _):
        @pl.when(i == 0)
        def _():
            part = slot.at[u, :, pl.ds(0, 3)]
            pltpu.make_async_copy(part, part, init_ss.at[u]).wait()

        @pl.when(spreads & (i > 0))
        def _():
            part = slot.at[u, :, pl.ds(0, 4)]
            pltpu.make_async_copy(part, part, init_ss.at[u]).wait()

        @pl.when(i < 7)
        def _():
            pltpu.make_async_copy(slot.at[u], slot.at[u], next_ss.at[u]).wait()
        sibling(u, 0).wait_send()

        @pl.when(d == 0)
        def _():
            sibling(u, 1).wait_send()
            partial(u).wait_send()
        three = obuf.at[u, pl.ds(0, 3)]
        pltpu.make_async_copy(three, three, out_ss.at[u]).wait()
        pltpu.make_async_copy(obuf.at[u, 0], obuf.at[u, 0], out_ls.at[u]).wait()
        return 0

    lax.fori_loop(0, UP_VALUES, drain, 0)
    pltpu.make_async_copy(out.at[pl.ds(0, 12)], out.at[pl.ds(0, 12)], out_rs).wait()


def on_device(env_in, mps, proj, mpo, mpo_charge, block_sizes):
    bf16 = jnp.bfloat16
    vm = pl.BlockSpec(memory_space=pltpu.VMEM)
    sm = pl.BlockSpec(memory_space=pltpu.SMEM)
    hbm = pl.BlockSpec(memory_space=pltpu.HBM)
    dma = pltpu.SemaphoreType.DMA
    out = pl.pallas_call(
        kernel,
        out_shape=jax.ShapeDtypeStruct((SECTORS, BLOCK, BLOCK), bf16),
        in_specs=[sm, sm, vm, hbm, hbm, hbm],
        out_specs=hbm,
        scratch_shapes=[
            pltpu.VMEM((UP_VALUES, 2, 16, 16, 256), bf16),
            pltpu.VMEM((2, 1024, 256), bf16),
            pltpu.VMEM((1024, 256), bf16),
            pltpu.VMEM((2, 4, HALF, BLOCK), jnp.float32),
            pltpu.VMEM((UP_VALUES, 2, 4, HALF, BLOCK), bf16),
            pltpu.VMEM((UP_VALUES, 2, 4, HALF, BLOCK), bf16),
            pltpu.VMEM((UP_VALUES, 4, HALF, BLOCK), bf16),
            pltpu.VMEM((UP_VALUES, 4, HALF, BLOCK), bf16),
            pltpu.VMEM((UP_VALUES, 2, 4, 16, 256), bf16),
            pltpu.VMEM((UP_VALUES, 4, HALF, BLOCK), bf16),
            pltpu.VMEM((2, 2, UP_VALUES, 2, 16, 256), bf16),
            pltpu.VMEM((UP_VALUES, 2, 2, BLOCK, BLOCK), bf16),
            pltpu.VMEM((UP_VALUES + 1, 2, 4, HALF, BLOCK), bf16),
            dma((8,)), dma((8,)), dma((8,)), dma((8, 2)), dma((8, 2)), dma((8,)), dma((8,)), dma((8,)), dma((8,)),
            dma((9,)), dma,
        ],
        compiler_params=pltpu.CompilerParams(collective_id=0, has_side_effects=True, vmem_limit_bytes=56 << 20),
        name="sweep",
    )(
        mpo_charge, block_sizes, mpo.reshape(64, 64),
        env_in.reshape(UP_VALUES, 2, 2, 2, 2, 16, BLOCK),
        mps.reshape(4, UP_VALUES, DOWN_VALUES, BLOCK, BLOCK),
        proj.reshape(4, UP_VALUES, DOWN_VALUES, BLOCK, BLOCK),
    )
    return out[None, None]


def solution(mesh):
    return jax.shard_map(
        on_device,
        mesh=mesh,
        in_specs=(
            P("op", None, None, None),
            P("chain", None, None, None, None),
            P("chain", None, None, None, None),
            P("chain", None, None, None, None),
            P(),
            P(),
        ),
        out_specs=P("chain", "op", None, None, None),
        check_vma=False,
    )
```

```python
import jax
import jax.numpy as jnp
from jax import lax
from jax.experimental import pallas as pl
from jax.experimental.pallas import tpu as pltpu
from jax.sharding import PartitionSpec as P

UP_VALUES = 8
DOWN_VALUES = 2
SECTORS = 16
BLOCK = 128
HALF = 64
MESH = pl.DeviceIdType.MESH

UP_CHARGE = (0, 1, 0, 1)
DOWN_CHARGE = (0, 0, 1, 1)
PHYS_ORDER = (0, 2, 1, 3)
INIT_ROUTES = ((0, 0, (0,)), (2, 0, (1, 3)), (6, 0, (2,)), (3, 1, (0, 3)), (7, 1, (1, 2)))


def role_of(op):
    y = op // 4
    return (op // 2) % 2 * 2 + y % 2, y // 2, op % 2


def op_of(group, down, half):
    return (down * 2 + group % 2) * 4 + group // 2 * 2 + half


def bond_of(group, member):
    return op_of(group, member // 2, member % 2)


def kernel(charge, sizes, coeff, env, mps, proj, out,
           slot, lbuf, mb, own, sib_s, sib_r, part_s, part_r, sbuf, obuf, env_r, mrows, pcols,
           slot_sem, next_ss, init_ss, sib_ss, sib_rs, part_ss, part_rs, out_ss, out_ls, load_sem, out_rs):
    i = lax.axis_index("chain")
    op = lax.axis_index("op")
    g, d, k = role_of(op)
    me = d * 2 + k
    f32, bf16 = jnp.float32, jnp.bfloat16

    bar = pltpu.get_barrier_semaphore()

    def near(step, flip, half):
        z = (op // 2) % 2
        z = 1 - z if flip else z
        return (op // 4 + step) % 4 * 4 + z * 2 + half

    def greet(chain, group, down, half):
        pl.semaphore_signal(bar, inc=1, device_id=(chain, op_of(group, down, half)), device_id_type=MESH)

    @pl.when(i > 0)
    def _():
        for j in range(4):
            greet(i - 1, (g + j) % 4, d, k)

    @pl.when(i == 0)
    def _():
        for source, flip, steps in INIT_ROUTES:
            for step in steps:
                for half in range(2):
                    if source or step:
                        pl.semaphore_signal(
                            bar, inc=1, device_id=(source, near(4 - step, flip, half)), device_id_type=MESH)
    greet(i, g, d, 1 - k)
    greet(i, g, 1 - d, k)
    greet(i, g, 1 - d, 1 - k)

    spreads = (i == 0) | (i == 2) | (i == 3) | (i > 5)

    @pl.when(spreads)
    def _():
        for down in range(2):
            for half in range(2):
                for side in range(2):
                    pltpu.make_async_copy(
                        env.at[:, down, half, :, side], env_r.at[down, half, :, :, :, pl.ds(side * BLOCK, BLOCK)],
                        load_sem.at[0]).start()

    def mps_load(p):
        up = UP_CHARGE[p]
        return pltpu.make_async_copy(
            mps.at[p, pl.ds(0, UP_VALUES - up), d], mrows.at[pl.ds(up, UP_VALUES - up), p // 2, up], load_sem.at[1 + p])

    def proj_load(t):
        up, down = UP_CHARGE[t], DOWN_CHARGE[t]
        return pltpu.make_async_copy(
            proj.at[t, pl.ds(0, UP_VALUES - up), pl.ds(0, DOWN_VALUES - down), pl.ds(k * HALF, HALF)],
            pcols.at[pl.ds(up, UP_VALUES - up), pl.ds(down, DOWN_VALUES - down), t], load_sem.at[5 + t])
    for p in range(4):
        mps_load(p).start()
        proj_load(p).start()
    zero = jnp.zeros((HALF, BLOCK), bf16)
    for t in range(4):
        pcols[UP_VALUES, 0, t] = zero
        for down in range(2):
            if UP_CHARGE[t]:
                pcols[0, down, t] = zero
        if DOWN_CHARGE[t]:
            for up in range(UP_CHARGE[t], UP_VALUES):
                pcols[up, 0, t] = zero
    for plane in range(2):
        mrows[0, plane, 1] = jnp.zeros((BLOCK, BLOCK), bf16)
    lbuf[...] = jnp.zeros_like(lbuf)

    rows = lax.broadcasted_iota(jnp.int32, (16, 64), 0)
    cols = lax.broadcasted_iota(jnp.int32, (16, 64), 1)
    pick = jnp.where(cols == bond_of(g, rows // 4) * 4 + rows % 4, 1.0, 0.0).astype(bf16)
    mine = lax.dot_general(pick, coeff[...], (((1,), (1,)), ((), ())), preferred_element_type=f32).astype(bf16)
    rows = lax.broadcasted_iota(jnp.int32, (16, 256), 0)
    cols = lax.broadcasted_iota(jnp.int32, (16, 256), 1)
    col_up = jnp.zeros((16, 256), jnp.int32)
    col_down = jnp.zeros((16, 256), jnp.int32)
    row_up = -(rows % 2)
    row_down = -((rows // 2) % 2)
    for n in range(16):
        b = bond_of(n // 4, n % 4)
        col_up = jnp.where(cols // 16 == n, charge[b, 0], col_up)
        col_down = jnp.where(cols // 16 == n, charge[b, 1], col_down)
    for m in range(4):
        b = bond_of(g, m)
        row_up = row_up + jnp.where(rows // 4 == m, charge[b, 0], 0)
        row_down = row_down + jnp.where(rows // 4 == m, charge[b, 1], 0)
    rows = lax.broadcasted_iota(jnp.int32, (64, 256), 0)
    cols = lax.broadcasted_iota(jnp.int32, (64, 256), 1)
    slot_bond = bond_of(cols // 64, cols // 16 % 4)
    long_rows = lax.broadcasted_iota(jnp.int32, (256, 256), 0)
    long_cols = lax.broadcasted_iota(jnp.int32, (256, 256), 1)
    repeat = jnp.where(
        lax.broadcasted_iota(jnp.int32, (256, 16), 0) // 16 == lax.broadcasted_iota(jnp.int32, (256, 16), 1),
        1.0, 0.0).astype(bf16)
    for place, p in enumerate(PHYS_ORDER):
        widen = jnp.where(rows == slot_bond * 4 + p, 1.0, 0.0).astype(bf16)
        wide = jnp.dot(mine, widen, preferred_element_type=f32)
        match = (col_up == row_up + UP_CHARGE[p]) & (col_down == row_down + DOWN_CHARGE[p])
        wide = jnp.where(match, wide, 0.0).astype(bf16)
        tall = jnp.dot(repeat, wide, preferred_element_type=f32)
        mb[place * 256:(place + 1) * 256, :] = jnp.where(long_rows % 16 == long_cols % 16, tall, 0.0).astype(bf16)

    @pl.when((i == 2) | (i == 3))
    def _():
        pl.semaphore_wait(bar, 11)

    @pl.when(i == 6)
    def _():
        pl.semaphore_wait(bar, 9)

    @pl.when((i < 2) | (i == 4) | (i == 5) | (i == 7))
    def _():
        pl.semaphore_wait(bar, 7)

    place = g * 4 + me

    @pl.when(spreads)
    def _():
        pltpu.make_async_copy(env_r, env_r, load_sem.at[0]).wait()

    def init_sent(u, count):
        part = slot.at[u, :, pl.ds(0, count)]
        pltpu.make_async_copy(part, part, init_ss.at[u]).wait()

    for source, flip, steps in INIT_ROUTES:
        def init_row(u, _):
            if source:
                @pl.when(u >= 2)
                def _():
                    init_sent(u - 2, 2 * len(steps))
            for step in steps:
                down = (op // 4 + step) % 4 // 2
                for half in range(2):
                    copy = pltpu.make_async_remote_copy(
                        env_r.at[down, half, u], slot.at[u, :, place], init_ss.at[u], slot_sem.at[u],
                        device_id=(0, near(step, flip, half)), device_id_type=MESH)
                    if source or step:
                        copy.start()
                    else:
                        @pl.when(half != k)
                        def _():
                            copy.start()
            if source == 0:
                pltpu.make_async_copy(env_r.at[d, k, u], slot.at[u, :, place], slot_sem.at[u]).start()
            return 0

        @pl.when(i == source)
        def _():
            lax.fori_loop(0, UP_VALUES, init_row, 0)
            if source:
                init_sent(UP_VALUES - 2, 2 * len(steps))
                init_sent(UP_VALUES - 1, 2 * len(steps))

    for p in range(4):
        mps_load(p).wait()
    rows = lax.broadcasted_iota(jnp.int32, (BLOCK, BLOCK), 0)
    cols = lax.broadcasted_iota(jnp.int32, (BLOCK, BLOCK), 1)

    def mask_row(u, _):
        for plane in range(2):
            for up in range(2):
                left = sizes[i, jnp.maximum(u - up, 0) * 2 + d]
                right = sizes[i + 1, u * 2 + jnp.minimum(d + plane, 1)]
                keep = (rows < left) & (cols < right)
                mrows[u, plane, up] = jnp.where(keep, mrows[u, plane, up].astype(f32), 0.0).astype(bf16)
        return 0
    lax.fori_loop(0, UP_VALUES, mask_row, 0)
    for t in range(4):
        proj_load(t).wait()

    def mix(u, first, planes):
        for pair in range(2):
            x = slot[u, pair].reshape(256, 256)
            y = jnp.dot(mb[first * 512:first * 512 + planes * 256, :], x, preferred_element_type=f32).astype(bf16)
            for side in range(2):
                for plane in range(planes):
                    lbuf[plane, pl.ds((2 * pair + side) * 256, 256), pl.ds(first * BLOCK, BLOCK)] = (
                        y[plane * 256:(plane + 1) * 256, side * BLOCK:(side + 1) * BLOCK])

    def apply(u, plane):
        grown = jnp.dot(lbuf[plane], mrows[u, plane].reshape(256, BLOCK), preferred_element_type=f32).astype(bf16)
        for m in range(4):
            b = bond_of(g, m)
            up = u + charge[b, 0]
            down = d + plane + charge[b, 1]
            inside = (up >= 0) & (up < UP_VALUES) & (down >= 0) & (down < DOWN_VALUES)
            up = jnp.where(inside, up, UP_VALUES)
            down = jnp.where(inside, down, 0)
            piece = jnp.concatenate(
                [grown[at * 256 + m * 64 + t * 16:at * 256 + m * 64 + t * 16 + 16] for t in range(4) for at in range(4)], axis=0)
            res = lax.dot_general(pcols[up, down].reshape(256, BLOCK), piece, (((0,), (0,)), ((), ())),
                                  preferred_element_type=f32)
            own[plane, m] = jnp.where(k == 0, res[:HALF], res[HALF:])
            sib_s[u, plane, m] = jnp.where(k == 0, res[HALF:], res[:HALF]).astype(bf16)

    def sibling(u, plane):
        return pltpu.make_async_remote_copy(
            sib_s.at[u, plane], sib_r.at[u, plane], sib_ss.at[u, plane], sib_rs.at[u, plane],
            device_id=(i, op_of(g, d, 1 - k)), device_id_type=MESH)

    def partial(u):
        return pltpu.make_async_remote_copy(
            part_s.at[u], part_r.at[u], part_ss.at[u], part_rs.at[u],
            device_id=(i, op_of(g, 1 - d, k)), device_id_type=MESH)

    def give(u, _):
        dst = out.at[u * 2 + d, pl.ds(k * HALF, HALF)]
        for j in range(1, 4):
            m = (me + j) % 4
            pltpu.make_async_remote_copy(
                obuf.at[u, m], dst, out_ss.at[u], out_rs,
                device_id=(i, bond_of(g, m)), device_id_type=MESH).start()
        pltpu.make_async_copy(obuf.at[u, me], dst, out_ls.at[u]).start()
        return 0

    def step(u, _):
        pltpu.make_async_copy(slot.at[u], slot.at[u], slot_sem.at[u]).wait()

        @pl.when(d == 0)
        def _():
            mix(u, 0, 2)

        @pl.when(d == 1)
        def _():
            mix(u, 0, 1)
        apply(u, 0)
        sibling(u, 0).start()

        @pl.when(d == 0)
        def _():
            apply(u, 1)
            sibling(u, 1).start()
            mix(u, 1, 2)

        @pl.when(d == 1)
        def _():
            mix(u, 1, 1)
        sibling(u, 0).wait_recv()

        @pl.when(d == 1)
        def _():
            partial(u).wait_recv()
            for m in range(4):
                own[0, m] = own[0, m] + part_r[u, m].astype(f32)

        for m in range(4):
            res = (own[0, m] + sib_r[u, 0, m].astype(f32)).astype(bf16)
            obuf[u, m] = res
            for pair in range(2):
                for side in range(2):
                    start = pair * 32 + side * 16
                    sbuf[u, pair, m, :, pl.ds(side * BLOCK, BLOCK)] = res[start:start + 16]

        @pl.when(i < 7)
        def _():
            for j in range(4):
                pltpu.make_async_remote_copy(
                    sbuf.at[u], slot.at[u, :, pl.ds(g * 4, 4)], next_ss.at[u], slot_sem.at[u],
                    device_id=(i + 1, op_of((g + j) % 4, d, k)), device_id_type=MESH).start()

        @pl.when(d == 0)
        def _():
            sibling(u, 1).wait_recv()
            for m in range(4):
                part_s[u, m] = (own[1, m] + sib_r[u, 1, m].astype(f32)).astype(bf16)
            partial(u).start()

        @pl.when(i == 7)
        def _():
            give(u, 0)
        return 0

    lax.fori_loop(0, UP_VALUES, step, 0)

    @pl.when(i < 7)
    def _():
        lax.fori_loop(0, UP_VALUES, give, 0)

    def drain(u, _):
        @pl.when(i == 0)
        def _():
            init_sent(u, 1)

        @pl.when(i < 7)
        def _():
            pltpu.make_async_copy(slot.at[u], slot.at[u], next_ss.at[u]).wait()
        sibling(u, 0).wait_send()

        @pl.when(d == 0)
        def _():
            sibling(u, 1).wait_send()
            partial(u).wait_send()
        three = obuf.at[u, pl.ds(0, 3)]
        pltpu.make_async_copy(three, three, out_ss.at[u]).wait()
        pltpu.make_async_copy(obuf.at[u, 0], obuf.at[u, 0], out_ls.at[u]).wait()
        return 0

    lax.fori_loop(0, UP_VALUES, drain, 0)
    pltpu.make_async_copy(out.at[pl.ds(0, 12)], out.at[pl.ds(0, 12)], out_rs).wait()


def on_device(env_in, mps, proj, mpo, mpo_charge, block_sizes):
    bf16 = jnp.bfloat16
    vm = pl.BlockSpec(memory_space=pltpu.VMEM)
    sm = pl.BlockSpec(memory_space=pltpu.SMEM)
    hbm = pl.BlockSpec(memory_space=pltpu.HBM)
    dma = pltpu.SemaphoreType.DMA
    out = pl.pallas_call(
        kernel,
        out_shape=jax.ShapeDtypeStruct((SECTORS, BLOCK, BLOCK), bf16),
        in_specs=[sm, sm, vm, hbm, hbm, hbm],
        out_specs=hbm,
        scratch_shapes=[
            pltpu.VMEM((UP_VALUES, 2, 16, 16, 256), bf16),
            pltpu.VMEM((2, 1024, 256), bf16),
            pltpu.VMEM((1024, 256), bf16),
            pltpu.VMEM((2, 4, HALF, BLOCK), jnp.float32),
            pltpu.VMEM((UP_VALUES, 2, 4, HALF, BLOCK), bf16),
            pltpu.VMEM((UP_VALUES, 2, 4, HALF, BLOCK), bf16),
            pltpu.VMEM((UP_VALUES, 4, HALF, BLOCK), bf16),
            pltpu.VMEM((UP_VALUES, 4, HALF, BLOCK), bf16),
            pltpu.VMEM((UP_VALUES, 2, 4, 16, 256), bf16),
            pltpu.VMEM((UP_VALUES, 4, HALF, BLOCK), bf16),
            pltpu.VMEM((2, 2, UP_VALUES, 2, 16, 256), bf16),
            pltpu.VMEM((UP_VALUES, 2, 2, BLOCK, BLOCK), bf16),
            pltpu.VMEM((UP_VALUES + 1, 2, 4, HALF, BLOCK), bf16),
            dma((8,)), dma((8,)), dma((8,)), dma((8, 2)), dma((8, 2)), dma((8,)), dma((8,)), dma((8,)), dma((8,)),
            dma((9,)), dma,
        ],
        compiler_params=pltpu.CompilerParams(collective_id=0, has_side_effects=True, vmem_limit_bytes=56 << 20),
        name="sweep",
    )(
        mpo_charge, block_sizes, mpo.reshape(64, 64),
        env_in.reshape(UP_VALUES, 2, 2, 2, 2, 16, BLOCK),
        mps.reshape(4, UP_VALUES, DOWN_VALUES, BLOCK, BLOCK),
        proj.reshape(4, UP_VALUES, DOWN_VALUES, BLOCK, BLOCK),
    )
    return out[None, None]


def solution(mesh):
    return jax.shard_map(
        on_device,
        mesh=mesh,
        in_specs=(
            P("op", None, None, None),
            P("chain", None, None, None, None),
            P("chain", None, None, None, None),
            P("chain", None, None, None, None),
            P(),
            P(),
        ),
        out_specs=P("chain", "op", None, None, None),
        check_vma=False,
    )
```

```python
import jax
import jax.numpy as jnp
from jax import lax
from jax.experimental import pallas as pl
from jax.experimental.pallas import tpu as pltpu
from jax.sharding import PartitionSpec as P

UP_VALUES = 8
DOWN_VALUES = 2
SECTORS = 16
BLOCK = 128
HALF = 64
MESH = pl.DeviceIdType.MESH

UP_CHARGE = (0, 1, 0, 1)
DOWN_CHARGE = (0, 0, 1, 1)
PHYS_ORDER = (0, 2, 1, 3)
INIT_ROUTES = ((0, 0, (0,)), (2, 0, (1, 3)), (6, 0, (2,)), (3, 1, (0, 3)), (7, 1, (1, 2)))


def role_of(op):
    y = op // 4
    return (op // 2) % 2 * 2 + y % 2, y // 2, op % 2


def op_of(group, down, half):
    return (down * 2 + group % 2) * 4 + group // 2 * 2 + half


def bond_of(group, member):
    return op_of(group, member // 2, member % 2)


def kernel(charge, sizes, coeff, env, mps, proj, out,
           slot, lbuf, mb, own, sib_s, sib_r, part_s, part_r, sbuf, obuf, env_r, mrows, pcols,
           slot_sem, next_ss, init_ss, sib_ss, sib_rs, part_ss, part_rs, out_ss, out_ls, load_sem, out_rs):
    i = lax.axis_index("chain")
    op = lax.axis_index("op")
    g, d, k = role_of(op)
    me = d * 2 + k
    f32, bf16 = jnp.float32, jnp.bfloat16

    bar = pltpu.get_barrier_semaphore()

    def near(step, flip, half):
        z = (op // 2) % 2
        z = 1 - z if flip else z
        return (op // 4 + step) % 4 * 4 + z * 2 + half

    def greet(chain, group, down, half):
        pl.semaphore_signal(bar, inc=1, device_id=(chain, op_of(group, down, half)), device_id_type=MESH)

    @pl.when(i > 0)
    def _():
        for j in range(4):
            greet(i - 1, (g + j) % 4, d, k)

    @pl.when(i == 0)
    def _():
        for source, flip, steps in INIT_ROUTES:
            for step in steps:
                for half in range(2):
                    if source or step:
                        pl.semaphore_signal(
                            bar, inc=1, device_id=(source, near(4 - step, flip, half)), device_id_type=MESH)
    greet(i, g, d, 1 - k)
    greet(i, g, 1 - d, k)
    greet(i, g, 1 - d, 1 - k)

    spreads = (i == 0) | (i == 2) | (i == 3) | (i > 5)

    @pl.when(spreads)
    def _():
        for down in range(2):
            for half in range(2):
                for side in range(2):
                    pltpu.make_async_copy(
                        env.at[:, down, half, :, side], env_r.at[down, half, :, :, :, pl.ds(side * BLOCK, BLOCK)],
                        load_sem.at[0]).start()

    def mps_load(p):
        up = UP_CHARGE[p]
        return pltpu.make_async_copy(
            mps.at[p, pl.ds(0, UP_VALUES - up), d], mrows.at[pl.ds(up, UP_VALUES - up), p // 2, up], load_sem.at[1 + p])

    def proj_load(t):
        up, down = UP_CHARGE[t], DOWN_CHARGE[t]
        return pltpu.make_async_copy(
            proj.at[t, pl.ds(0, UP_VALUES - up), pl.ds(0, DOWN_VALUES - down), pl.ds(k * HALF, HALF)],
            pcols.at[pl.ds(up, UP_VALUES - up), pl.ds(down, DOWN_VALUES - down), t], load_sem.at[5 + t])
    for p in range(4):
        mps_load(p).start()
        proj_load(p).start()
    for count, sites in ((7, (0, 1, 4, 5, 7)), (11, (2, 3)), (9, (6,))):
        here = i == sites[0]
        for other in sites[1:]:
            here = here | (i == other)

        @pl.when(here)
        def _():
            pl.semaphore_wait(bar, count)

    place = g * 4 + me

    @pl.when(spreads)
    def _():
        pltpu.make_async_copy(env_r, env_r, load_sem.at[0]).wait()

    def init_sent(u, count):
        part = slot.at[u, :, pl.ds(0, count)]
        pltpu.make_async_copy(part, part, init_ss.at[u]).wait()

    def spread(first, last):
        for source, flip, steps in INIT_ROUTES:
            def init_row(u, _):
                if source and first:
                    init_sent(u - 2, 2 * len(steps))
                for step in steps:
                    down = (op // 4 + step) % 4 // 2
                    for half in range(2):
                        copy = pltpu.make_async_remote_copy(
                            env_r.at[down, half, u], slot.at[u, :, place], init_ss.at[u], slot_sem.at[u],
                            device_id=(0, near(step, flip, half)), device_id_type=MESH)
                        if source or step:
                            copy.start()
                        else:
                            @pl.when(half != k)
                            def _():
                                copy.start()
                if source == 0:
                    pltpu.make_async_copy(env_r.at[d, k, u], slot.at[u, :, place], slot_sem.at[u]).start()
                return 0

            @pl.when(i == source)
            def _():
                lax.fori_loop(first, last, init_row, 0)
                if source and first:
                    init_sent(UP_VALUES - 2, 2 * len(steps))
                    init_sent(UP_VALUES - 1, 2 * len(steps))

    spread(0, 2)
    zero = jnp.zeros((HALF, BLOCK), bf16)
    for t in range(4):
        pcols[UP_VALUES, 0, t] = zero
        for down in range(2):
            if UP_CHARGE[t]:
                pcols[0, down, t] = zero
        if DOWN_CHARGE[t]:
            for up in range(UP_CHARGE[t], UP_VALUES):
                pcols[up, 0, t] = zero
    for plane in range(2):
        mrows[0, plane, 1] = jnp.zeros((BLOCK, BLOCK), bf16)
    lbuf[2] = jnp.zeros((2, 1024, BLOCK), bf16)

    rows = lax.broadcasted_iota(jnp.int32, (16, 64), 0)
    cols = lax.broadcasted_iota(jnp.int32, (16, 64), 1)
    pick = jnp.where(cols == bond_of(g, rows // 4) * 4 + rows % 4, 1.0, 0.0).astype(bf16)
    mine = lax.dot_general(pick, coeff[...], (((1,), (1,)), ((), ())), preferred_element_type=f32).astype(bf16)
    rows = lax.broadcasted_iota(jnp.int32, (16, 256), 0)
    cols = lax.broadcasted_iota(jnp.int32, (16, 256), 1)
    col_up = jnp.zeros((16, 256), jnp.int32)
    col_down = jnp.zeros((16, 256), jnp.int32)
    row_up = -(rows % 2)
    row_down = -((rows // 2) % 2)
    for n in range(16):
        b = bond_of(n // 4, n % 4)
        col_up = jnp.where(cols // 16 == n, charge[b, 0], col_up)
        col_down = jnp.where(cols // 16 == n, charge[b, 1], col_down)
    for m in range(4):
        b = bond_of(g, m)
        row_up = row_up + jnp.where(rows // 4 == m, charge[b, 0], 0)
        row_down = row_down + jnp.where(rows // 4 == m, charge[b, 1], 0)
    rows = lax.broadcasted_iota(jnp.int32, (64, 256), 0)
    cols = lax.broadcasted_iota(jnp.int32, (64, 256), 1)
    slot_bond = bond_of(cols // 64, cols // 16 % 4)
    long_rows = lax.broadcasted_iota(jnp.int32, (256, 256), 0)
    long_cols = lax.broadcasted_iota(jnp.int32, (256, 256), 1)
    repeat = jnp.where(
        lax.broadcasted_iota(jnp.int32, (256, 16), 0) // 16 == lax.broadcasted_iota(jnp.int32, (256, 16), 1),
        1.0, 0.0).astype(bf16)
    for rank, p in enumerate(PHYS_ORDER):
        widen = jnp.where(rows == slot_bond * 4 + p, 1.0, 0.0).astype(bf16)
        wide = jnp.dot(mine, widen, preferred_element_type=f32)
        match = (col_up == row_up + UP_CHARGE[p]) & (col_down == row_down + DOWN_CHARGE[p])
        wide = jnp.where(match, wide, 0.0).astype(bf16)
        tall = jnp.dot(repeat, wide, preferred_element_type=f32)
        mb[rank * 256:(rank + 1) * 256, :] = jnp.where(long_rows % 16 == long_cols % 16, tall, 0.0).astype(bf16)

    for p in range(4):
        mps_load(p).wait()
    rows = lax.broadcasted_iota(jnp.int32, (BLOCK, BLOCK), 0)
    cols = lax.broadcasted_iota(jnp.int32, (BLOCK, BLOCK), 1)

    def mask_row(u, _):
        for plane in range(2):
            for up in range(2):
                left = sizes[i, jnp.maximum(u - up, 0) * 2 + d]
                right = sizes[i + 1, u * 2 + jnp.minimum(d + plane, 1)]
                keep = (rows < left) & (cols < right)
                mrows[u, plane, up] = jnp.where(keep, mrows[u, plane, up].astype(f32), 0.0).astype(bf16)
        return 0
    lax.fori_loop(0, UP_VALUES, mask_row, 0)
    for t in range(4):
        proj_load(t).wait()
    spread(2, UP_VALUES)

    def mix(u, first):
        place = first * (1 + u % 2)
        for pair in range(2):
            x = slot[u, pair].reshape(256, 256)
            y = jnp.dot(mb[pl.ds(pl.multiple_of(first * 512, 512), 512), :], x, preferred_element_type=f32).astype(bf16)
            for side in range(2):
                for plane in range(2):
                    lbuf[place, plane, pl.ds((2 * pair + side) * 256, 256)] = (
                        y[plane * 256:(plane + 1) * 256, side * BLOCK:(side + 1) * BLOCK])

    def apply(u, plane):
        both = jnp.concatenate([lbuf[0, plane], lbuf[1 + (u + 1) % 2, plane]], axis=1)
        grown = jnp.dot(both, mrows[u, plane].reshape(256, BLOCK), preferred_element_type=f32).astype(bf16)
        for m in range(4):
            b = bond_of(g, m)
            up = u + charge[b, 0]
            down = d + plane + charge[b, 1]
            inside = (up >= 0) & (up < UP_VALUES) & (down >= 0) & (down < DOWN_VALUES)
            up = jnp.where(inside, up, UP_VALUES)
            down = jnp.where(inside, down, 0)
            piece = jnp.concatenate(
                [grown[at * 256 + m * 64 + t * 16:at * 256 + m * 64 + t * 16 + 16] for t in range(4) for at in range(4)], axis=0)
            res = lax.dot_general(pcols[up, down].reshape(256, BLOCK), piece, (((0,), (0,)), ((), ())),
                                  preferred_element_type=f32)
            own[plane, m] = jnp.where(k == 0, res[:HALF], res[HALF:])
            sib_s[u, plane, m] = jnp.where(k == 0, res[HALF:], res[:HALF]).astype(bf16)

    def sibling(u, plane):
        return pltpu.make_async_remote_copy(
            sib_s.at[u, plane], sib_r.at[u, plane], sib_ss.at[u, plane], sib_rs.at[u, plane],
            device_id=(i, op_of(g, d, 1 - k)), device_id_type=MESH)

    def partial(u):
        return pltpu.make_async_remote_copy(
            part_s.at[u], part_r.at[u], part_ss.at[u], part_rs.at[u],
            device_id=(i, op_of(g, 1 - d, k)), device_id_type=MESH)

    def to_next(u, group):
        return pltpu.make_async_remote_copy(
            sbuf.at[u], slot.at[u, :, pl.ds(g * 4, 4)], next_ss.at[u], slot_sem.at[u],
            device_id=(i + 1, op_of(group, d, k)), device_id_type=MESH)

    def hand_over(u):
        sibling(u, 1).wait_recv()
        for m in range(4):
            part_s[u, m] = (own[1, m] + sib_r[u, 1, m].astype(f32)).astype(bf16)
        partial(u).start()

    def finish(u):
        sibling(u, 0).wait_recv()

        @pl.when(d == 1)
        def _():
            partial(u).wait_recv()
            for m in range(4):
                own[0, m] = own[0, m] + part_r[u, m].astype(f32)

        for m in range(4):
            res = (own[0, m] + sib_r[u, 0, m].astype(f32)).astype(bf16)
            obuf[m, u] = res
            for pair in range(2):
                for side in range(2):
                    start = pair * 32 + side * 16
                    sbuf[u, pair, m, :, pl.ds(side * BLOCK, BLOCK)] = res[start:start + 16]

        @pl.when(i < 7)
        def _():
            for j in range(4):
                to_next(u, (g + j) % 4).start()

        @pl.when(i > 5)
        def _():
            for j in range(1, 4):
                m = (me + j) % 4
                pltpu.make_async_remote_copy(
                    obuf.at[m, u], out.at[u, d, k], out_ss.at[u], out_rs,
                    device_id=(i, bond_of(g, m)), device_id_type=MESH).start()
            pltpu.make_async_copy(obuf.at[me, u], out.at[u, d, k], out_ls.at[u]).start()

    def step(n, _):
        u, plane = n // 2, n % 2

        @pl.when(plane == 0)
        def _():
            pltpu.make_async_copy(slot.at[u], slot.at[u], slot_sem.at[u]).wait()

        @pl.when(n < 2 * UP_VALUES - 1)
        def _():
            mix(u, plane)

        @pl.when((plane == 0) | (d == 0))
        def _():
            apply(u, plane)
            sibling(u, plane).start()

        @pl.when(plane == 0)
        def _():
            finish(u)

        @pl.when((plane == 1) & (d == 0))
        def _():
            hand_over(u)
        return 0

    lax.fori_loop(0, 2 * UP_VALUES, step, 0)

    @pl.when(i < 6)
    def _():
        for j in range(1, 4):
            m = (me + j) % 4
            pltpu.make_async_remote_copy(
                obuf.at[m], out.at[:, d, k], out_ss.at[0], out_rs,
                device_id=(i, bond_of(g, m)), device_id_type=MESH).start()
        pltpu.make_async_copy(obuf.at[me], out.at[:, d, k], out_ls.at[0]).start()
        pltpu.make_async_copy(obuf.at[pl.ds(0, 3)], obuf.at[pl.ds(0, 3)], out_ss.at[0]).wait()
        pltpu.make_async_copy(obuf.at[0], obuf.at[0], out_ls.at[0]).wait()

    def drain(u, _):
        @pl.when(i == 0)
        def _():
            init_sent(u, 1)

        @pl.when(i < 7)
        def _():
            pltpu.make_async_copy(slot.at[u], slot.at[u], next_ss.at[u]).wait()
        sibling(u, 0).wait_send()

        @pl.when(d == 0)
        def _():
            sibling(u, 1).wait_send()
            partial(u).wait_send()

        @pl.when(i > 5)
        def _():
            three = obuf.at[pl.ds(0, 3), u]
            pltpu.make_async_copy(three, three, out_ss.at[u]).wait()
            pltpu.make_async_copy(obuf.at[0, u], obuf.at[0, u], out_ls.at[u]).wait()
        return 0

    lax.fori_loop(0, UP_VALUES, drain, 0)
    pltpu.make_async_copy(out.at[pl.ds(0, 6)], out.at[pl.ds(0, 6)], out_rs).wait()


def on_device(env_in, mps, proj, mpo, mpo_charge, block_sizes):
    bf16 = jnp.bfloat16
    vm = pl.BlockSpec(memory_space=pltpu.VMEM)
    sm = pl.BlockSpec(memory_space=pltpu.SMEM)
    hbm = pl.BlockSpec(memory_space=pltpu.HBM)
    dma = pltpu.SemaphoreType.DMA
    out = pl.pallas_call(
        kernel,
        out_shape=jax.ShapeDtypeStruct((UP_VALUES, DOWN_VALUES, 2, HALF, BLOCK), bf16),
        in_specs=[sm, sm, vm, hbm, hbm, hbm],
        out_specs=hbm,
        scratch_shapes=[
            pltpu.VMEM((UP_VALUES, 2, 16, 16, 256), bf16),
            pltpu.VMEM((3, 2, 1024, BLOCK), bf16),
            pltpu.VMEM((1024, 256), bf16),
            pltpu.VMEM((2, 4, HALF, BLOCK), jnp.float32),
            pltpu.VMEM((UP_VALUES, 2, 4, HALF, BLOCK), bf16),
            pltpu.VMEM((UP_VALUES, 2, 4, HALF, BLOCK), bf16),
            pltpu.VMEM((UP_VALUES, 4, HALF, BLOCK), bf16),
            pltpu.VMEM((UP_VALUES, 4, HALF, BLOCK), bf16),
            pltpu.VMEM((UP_VALUES, 2, 4, 16, 256), bf16),
            pltpu.VMEM((4, UP_VALUES, HALF, BLOCK), bf16),
            pltpu.VMEM((2, 2, UP_VALUES, 2, 16, 256), bf16),
            pltpu.VMEM((UP_VALUES, 2, 2, BLOCK, BLOCK), bf16),
            pltpu.VMEM((UP_VALUES + 1, 2, 4, HALF, BLOCK), bf16),
            dma((8,)), dma((8,)), dma((8,)), dma((8, 2)), dma((8, 2)), dma((8,)), dma((8,)), dma((8,)), dma((8,)),
            dma((9,)), dma,
        ],
        compiler_params=pltpu.CompilerParams(collective_id=0, has_side_effects=True, vmem_limit_bytes=56 << 20),
        name="sweep",
    )(
        mpo_charge, block_sizes, mpo.reshape(64, 64),
        env_in.reshape(UP_VALUES, 2, 2, 2, 2, 16, BLOCK),
        mps.reshape(4, UP_VALUES, DOWN_VALUES, BLOCK, BLOCK),
        proj.reshape(4, UP_VALUES, DOWN_VALUES, BLOCK, BLOCK),
    )
    return out.reshape(1, 1, SECTORS, BLOCK, BLOCK)


def solution(mesh):
    return jax.shard_map(
        on_device,
        mesh=mesh,
        in_specs=(
            P("op", None, None, None),
            P("chain", None, None, None, None),
            P("chain", None, None, None, None),
            P("chain", None, None, None, None),
            P(),
            P(),
        ),
        out_specs=P("chain", "op", None, None, None),
        check_vma=False,
    )
```

```python
import jax
import jax.numpy as jnp
from jax import lax
from jax.experimental import pallas as pl
from jax.experimental.pallas import tpu as pltpu
from jax.sharding import PartitionSpec as P

UP_VALUES = 8
DOWN_VALUES = 2
SECTORS = 16
BLOCK = 128
HALF = 64
MESH = pl.DeviceIdType.MESH

UP_CHARGE = (0, 1, 0, 1)
DOWN_CHARGE = (0, 0, 1, 1)
PHYS_ORDER = (0, 2, 1, 3)
INIT_ROUTES = ((0, 0, (0,)), (2, 0, (1, 3)), (6, 0, (2,)), (3, 1, (0, 3)), (7, 1, (1, 2)))


def role_of(op):
    y = op // 4
    return (op // 2) % 2 * 2 + y % 2, y // 2, op % 2


def op_of(group, down, half):
    return (down * 2 + group % 2) * 4 + group // 2 * 2 + half


def bond_of(group, member):
    return op_of(group, member // 2, member % 2)


def kernel(charge, sizes, coeff, env, mps, proj, out,
           slot, lbuf, mb, own, sib_s, sib_r, part_s, part_r, sbuf, obuf, env_r, mrows, pcols,
           slot_sem, next_ss, init_ss, sib_ss, sib_rs, part_ss, part_rs, out_ss, out_ls, load_sem, out_rs):
    i = lax.axis_index("chain")
    op = lax.axis_index("op")
    g, d, k = role_of(op)
    me = d * 2 + k
    f32, bf16 = jnp.float32, jnp.bfloat16

    bar = pltpu.get_barrier_semaphore()

    def near(step, flip, half):
        z = (op // 2) % 2
        z = 1 - z if flip else z
        return (op // 4 + step) % 4 * 4 + z * 2 + half

    def greet(chain, group, down, half):
        pl.semaphore_signal(bar, inc=1, device_id=(chain, op_of(group, down, half)), device_id_type=MESH)

    @pl.when(i > 0)
    def _():
        for j in range(4):
            greet(i - 1, (g + j) % 4, d, k)

    @pl.when(i == 0)
    def _():
        for source, flip, steps in INIT_ROUTES:
            for step in steps:
                for half in range(2):
                    if source or step:
                        pl.semaphore_signal(
                            bar, inc=1, device_id=(source, near(4 - step, flip, half)), device_id_type=MESH)
    greet(i, g, d, 1 - k)
    greet(i, g, 1 - d, k)
    greet(i, g, 1 - d, 1 - k)

    spreads = (i == 0) | (i == 2) | (i == 3) | (i > 5)

    @pl.when(spreads)
    def _():
        for down in range(2):
            for half in range(2):
                for side in range(2):
                    pltpu.make_async_copy(
                        env.at[:, down, half, :, side], env_r.at[down, half, :, :, :, pl.ds(side * BLOCK, BLOCK)],
                        load_sem.at[0]).start()

    def mps_load(p):
        up = UP_CHARGE[p]
        return pltpu.make_async_copy(
            mps.at[p, pl.ds(0, UP_VALUES - up), d], mrows.at[pl.ds(up, UP_VALUES - up), p // 2, up], load_sem.at[1 + p])

    def proj_load(t):
        up, down = UP_CHARGE[t], DOWN_CHARGE[t]
        return pltpu.make_async_copy(
            proj.at[t, pl.ds(0, UP_VALUES - up), pl.ds(0, DOWN_VALUES - down), pl.ds(k * HALF, HALF)],
            pcols.at[pl.ds(up, UP_VALUES - up), pl.ds(down, DOWN_VALUES - down), t], load_sem.at[5 + t])
    for p in range(4):
        mps_load(p).start()
        proj_load(p).start()
    for count, sites in ((7, (0, 1, 4, 5, 7)), (11, (2, 3)), (9, (6,))):
        here = i == sites[0]
        for other in sites[1:]:
            here = here | (i == other)

        @pl.when(here)
        def _():
            pl.semaphore_wait(bar, count)

    place = g * 4 + me

    @pl.when(spreads)
    def _():
        pltpu.make_async_copy(env_r, env_r, load_sem.at[0]).wait()

    def init_sent(u, count):
        part = slot.at[u, :, pl.ds(0, count)]
        pltpu.make_async_copy(part, part, init_ss.at[u]).wait()

    def spread(first, last):
        for source, flip, steps in INIT_ROUTES:
            def init_row(u, _):
                if source and first:
                    init_sent(u - 2, 2 * len(steps))
                for step in steps:
                    down = (op // 4 + step) % 4 // 2
                    for half in range(2):
                        copy = pltpu.make_async_remote_copy(
                            env_r.at[down, half, u], slot.at[u, :, place], init_ss.at[u], slot_sem.at[u],
                            device_id=(0, near(step, flip, half)), device_id_type=MESH)
                        if source or step:
                            copy.start()
                        else:
                            @pl.when(half != k)
                            def _():
                                copy.start()
                if source == 0:
                    pltpu.make_async_copy(env_r.at[d, k, u], slot.at[u, :, place], slot_sem.at[u]).start()
                return 0

            @pl.when(i == source)
            def _():
                lax.fori_loop(first, last, init_row, 0)
                if source and first:
                    init_sent(UP_VALUES - 2, 2 * len(steps))
                    init_sent(UP_VALUES - 1, 2 * len(steps))

    spread(0, 2)
    zero = jnp.zeros((HALF, BLOCK), bf16)
    for t in range(4):
        pcols[UP_VALUES, 0, t] = zero
        for down in range(2):
            if UP_CHARGE[t]:
                pcols[0, down, t] = zero
        if DOWN_CHARGE[t]:
            for up in range(UP_CHARGE[t], UP_VALUES):
                pcols[up, 0, t] = zero
    for plane in range(2):
        mrows[0, plane, 1] = jnp.zeros((BLOCK, BLOCK), bf16)
    lbuf[2] = jnp.zeros((2, 1024, BLOCK), bf16)

    rows = lax.broadcasted_iota(jnp.int32, (16, 64), 0)
    cols = lax.broadcasted_iota(jnp.int32, (16, 64), 1)
    pick = jnp.where(cols == bond_of(g, rows // 4) * 4 + rows % 4, 1.0, 0.0).astype(bf16)
    mine = lax.dot_general(pick, coeff[...], (((1,), (1,)), ((), ())), preferred_element_type=f32).astype(bf16)
    rows = lax.broadcasted_iota(jnp.int32, (16, 256), 0)
    cols = lax.broadcasted_iota(jnp.int32, (16, 256), 1)
    col_up = jnp.zeros((16, 256), jnp.int32)
    col_down = jnp.zeros((16, 256), jnp.int32)
    row_up = -(rows % 2)
    row_down = -((rows // 2) % 2)
    for n in range(16):
        b = bond_of(n // 4, n % 4)
        col_up = jnp.where(cols // 16 == n, charge[b, 0], col_up)
        col_down = jnp.where(cols // 16 == n, charge[b, 1], col_down)
    for m in range(4):
        b = bond_of(g, m)
        row_up = row_up + jnp.where(rows // 4 == m, charge[b, 0], 0)
        row_down = row_down + jnp.where(rows // 4 == m, charge[b, 1], 0)
    rows = lax.broadcasted_iota(jnp.int32, (64, 256), 0)
    cols = lax.broadcasted_iota(jnp.int32, (64, 256), 1)
    slot_bond = bond_of(cols // 64, cols // 16 % 4)
    long_rows = lax.broadcasted_iota(jnp.int32, (256, 256), 0)
    long_cols = lax.broadcasted_iota(jnp.int32, (256, 256), 1)
    repeat = jnp.where(
        lax.broadcasted_iota(jnp.int32, (256, 16), 0) // 16 == lax.broadcasted_iota(jnp.int32, (256, 16), 1),
        1.0, 0.0).astype(bf16)
    for rank, p in enumerate(PHYS_ORDER):
        widen = jnp.where(rows == slot_bond * 4 + p, 1.0, 0.0).astype(bf16)
        wide = jnp.dot(mine, widen, preferred_element_type=f32)
        match = (col_up == row_up + UP_CHARGE[p]) & (col_down == row_down + DOWN_CHARGE[p])
        wide = jnp.where(match, wide, 0.0).astype(bf16)
        tall = jnp.dot(repeat, wide, preferred_element_type=f32)
        mb[rank * 256:(rank + 1) * 256, :] = jnp.where(long_rows % 16 == long_cols % 16, tall, 0.0).astype(bf16)

    for p in range(4):
        mps_load(p).wait()
    rows = lax.broadcasted_iota(jnp.int32, (BLOCK, BLOCK), 0)
    cols = lax.broadcasted_iota(jnp.int32, (BLOCK, BLOCK), 1)

    def mask_row(u, _):
        for plane in range(2):
            for up in range(2):
                left = sizes[i, jnp.maximum(u - up, 0) * 2 + d]
                right = sizes[i + 1, u * 2 + jnp.minimum(d + plane, 1)]
                keep = (rows < left) & (cols < right)
                mrows[u, plane, up] = jnp.where(keep, mrows[u, plane, up].astype(f32), 0.0).astype(bf16)
        return 0
    lax.fori_loop(0, UP_VALUES, mask_row, 0)
    for t in range(4):
        proj_load(t).wait()
    spread(2, UP_VALUES)

    def mix(u, first):
        place = first * (1 + u % 2)
        for pair in range(2):
            x = slot[u, pair].reshape(256, 256)
            y = jnp.dot(mb[pl.ds(pl.multiple_of(first * 512, 512), 512), :], x, preferred_element_type=f32).astype(bf16)
            for side in range(2):
                for plane in range(2):
                    lbuf[place, plane, pl.ds((2 * pair + side) * 256, 256)] = (
                        y[plane * 256:(plane + 1) * 256, side * BLOCK:(side + 1) * BLOCK])

    def apply(u, plane):
        both = jnp.concatenate([lbuf[0, plane], lbuf[1 + (u + 1) % 2, plane]], axis=1)
        grown = jnp.dot(both, mrows[u, plane].reshape(256, BLOCK), preferred_element_type=f32).astype(bf16)
        for m in range(4):
            b = bond_of(g, m)
            up = u + charge[b, 0]
            down = d + plane + charge[b, 1]
            inside = (up >= 0) & (up < UP_VALUES) & (down >= 0) & (down < DOWN_VALUES)
            up = jnp.where(inside, up, UP_VALUES)
            down = jnp.where(inside, down, 0)
            piece = jnp.concatenate(
                [grown[at * 256 + m * 64 + t * 16:at * 256 + m * 64 + t * 16 + 16] for t in range(4) for at in range(4)], axis=0)
            res = lax.dot_general(pcols[up, down].reshape(256, BLOCK), piece, (((0,), (0,)), ((), ())),
                                  preferred_element_type=f32)
            own[plane, m] = jnp.where(k == 0, res[:HALF], res[HALF:])
            sib_s[u, plane, m] = jnp.where(k == 0, res[HALF:], res[:HALF]).astype(bf16)

    def sibling(u, plane):
        return pltpu.make_async_remote_copy(
            sib_s.at[u, plane], sib_r.at[u, plane], sib_ss.at[u, plane], sib_rs.at[u, plane],
            device_id=(i, op_of(g, d, 1 - k)), device_id_type=MESH)

    def partial(u):
        return pltpu.make_async_remote_copy(
            part_s.at[u], part_r.at[u], part_ss.at[u], part_rs.at[u],
            device_id=(i, op_of(g, 1 - d, k)), device_id_type=MESH)

    def to_next(u, group):
        return pltpu.make_async_remote_copy(
            sbuf.at[u], slot.at[u, :, pl.ds(g * 4, 4)], next_ss.at[u], slot_sem.at[u],
            device_id=(i + 1, op_of(group, d, k)), device_id_type=MESH)

    def hand_over(u):
        sibling(u, 1).wait_recv()
        for m in range(4):
            part_s[u, m] = (own[1, m] + sib_r[u, 1, m].astype(f32)).astype(bf16)
        partial(u).start()

    def finish(u):
        sibling(u, 0).wait_recv()

        @pl.when(d == 1)
        def _():
            partial(u).wait_recv()
            for m in range(4):
                own[0, m] = own[0, m] + part_r[u, m].astype(f32)

        for m in range(4):
            res = (own[0, m] + sib_r[u, 0, m].astype(f32)).astype(bf16)
            obuf[m, u] = res
            for pair in range(2):
                for side in range(2):
                    start = pair * 32 + side * 16
                    sbuf[u, pair, m, :, pl.ds(side * BLOCK, BLOCK)] = res[start:start + 16]

        @pl.when(i < 7)
        def _():
            for flip_z, flip_y in ((1, 1), (0, 1), (1, 0), (0, 0)):
                z = g // 2 + flip_z * (1 - 2 * (g // 2))
                y = g % 2 + flip_y * (1 - 2 * (g % 2))
                to_next(u, z * 2 + y).start()

        @pl.when(i > 5)
        def _():
            for j in range(1, 4):
                m = (me + j) % 4
                pltpu.make_async_remote_copy(
                    obuf.at[m, u], out.at[u, d, k], out_ss.at[u], out_rs,
                    device_id=(i, bond_of(g, m)), device_id_type=MESH).start()
            pltpu.make_async_copy(obuf.at[me, u], out.at[u, d, k], out_ls.at[u]).start()

    def step(n, _):
        u, plane = n // 2, n % 2

        @pl.when(plane == 0)
        def _():
            pltpu.make_async_copy(slot.at[u], slot.at[u], slot_sem.at[u]).wait()

        @pl.when(n < 2 * UP_VALUES - 1)
        def _():
            mix(u, plane)

        @pl.when((plane == 0) | (d == 0))
        def _():
            apply(u, plane)
            sibling(u, plane).start()

        @pl.when(plane == 0)
        def _():
            finish(u)

        @pl.when((plane == 1) & (d == 0))
        def _():
            hand_over(u)
        return 0

    lax.fori_loop(0, 2 * UP_VALUES, step, 0)

    @pl.when(i < 6)
    def _():
        for j in range(1, 4):
            m = (me + j) % 4
            pltpu.make_async_remote_copy(
                obuf.at[m], out.at[:, d, k], out_ss.at[0], out_rs,
                device_id=(i, bond_of(g, m)), device_id_type=MESH).start()
        pltpu.make_async_copy(obuf.at[me], out.at[:, d, k], out_ls.at[0]).start()
        pltpu.make_async_copy(obuf.at[pl.ds(0, 3)], obuf.at[pl.ds(0, 3)], out_ss.at[0]).wait()
        pltpu.make_async_copy(obuf.at[0], obuf.at[0], out_ls.at[0]).wait()

    def drain(u, _):
        @pl.when(i == 0)
        def _():
            init_sent(u, 1)

        @pl.when(i < 7)
        def _():
            pltpu.make_async_copy(slot.at[u], slot.at[u], next_ss.at[u]).wait()
        sibling(u, 0).wait_send()

        @pl.when(d == 0)
        def _():
            sibling(u, 1).wait_send()
            partial(u).wait_send()

        @pl.when(i > 5)
        def _():
            three = obuf.at[pl.ds(0, 3), u]
            pltpu.make_async_copy(three, three, out_ss.at[u]).wait()
            pltpu.make_async_copy(obuf.at[0, u], obuf.at[0, u], out_ls.at[u]).wait()
        return 0

    lax.fori_loop(0, UP_VALUES, drain, 0)
    pltpu.make_async_copy(out.at[pl.ds(0, 6)], out.at[pl.ds(0, 6)], out_rs).wait()


def on_device(env_in, mps, proj, mpo, mpo_charge, block_sizes):
    bf16 = jnp.bfloat16
    vm = pl.BlockSpec(memory_space=pltpu.VMEM)
    sm = pl.BlockSpec(memory_space=pltpu.SMEM)
    hbm = pl.BlockSpec(memory_space=pltpu.HBM)
    dma = pltpu.SemaphoreType.DMA
    out = pl.pallas_call(
        kernel,
        out_shape=jax.ShapeDtypeStruct((UP_VALUES, DOWN_VALUES, 2, HALF, BLOCK), bf16),
        in_specs=[sm, sm, vm, hbm, hbm, hbm],
        out_specs=hbm,
        scratch_shapes=[
            pltpu.VMEM((UP_VALUES, 2, 16, 16, 256), bf16),
            pltpu.VMEM((3, 2, 1024, BLOCK), bf16),
            pltpu.VMEM((1024, 256), bf16),
            pltpu.VMEM((2, 4, HALF, BLOCK), jnp.float32),
            pltpu.VMEM((UP_VALUES, 2, 4, HALF, BLOCK), bf16),
            pltpu.VMEM((UP_VALUES, 2, 4, HALF, BLOCK), bf16),
            pltpu.VMEM((UP_VALUES, 4, HALF, BLOCK), bf16),
            pltpu.VMEM((UP_VALUES, 4, HALF, BLOCK), bf16),
            pltpu.VMEM((UP_VALUES, 2, 4, 16, 256), bf16),
            pltpu.VMEM((4, UP_VALUES, HALF, BLOCK), bf16),
            pltpu.VMEM((2, 2, UP_VALUES, 2, 16, 256), bf16),
            pltpu.VMEM((UP_VALUES, 2, 2, BLOCK, BLOCK), bf16),
            pltpu.VMEM((UP_VALUES + 1, 2, 4, HALF, BLOCK), bf16),
            dma((8,)), dma((8,)), dma((8,)), dma((8, 2)), dma((8, 2)), dma((8,)), dma((8,)), dma((8,)), dma((8,)),
            dma((9,)), dma,
        ],
        compiler_params=pltpu.CompilerParams(collective_id=0, has_side_effects=True, vmem_limit_bytes=53 << 20),
        name="sweep",
    )(
        mpo_charge, block_sizes, mpo.reshape(64, 64),
        env_in.reshape(UP_VALUES, 2, 2, 2, 2, 16, BLOCK),
        mps.reshape(4, UP_VALUES, DOWN_VALUES, BLOCK, BLOCK),
        proj.reshape(4, UP_VALUES, DOWN_VALUES, BLOCK, BLOCK),
    )
    return out.reshape(1, 1, SECTORS, BLOCK, BLOCK)


def solution(mesh):
    return jax.shard_map(
        on_device,
        mesh=mesh,
        in_specs=(
            P("op", None, None, None),
            P("chain", None, None, None, None),
            P("chain", None, None, None, None),
            P("chain", None, None, None, None),
            P(),
            P(),
        ),
        out_specs=P("chain", "op", None, None, None),
        check_vma=False,
    )
```

```python
import jax
import jax.numpy as jnp
from jax import lax
from jax.experimental import pallas as pl
from jax.experimental.pallas import tpu as pltpu
from jax.sharding import PartitionSpec as P

UP_VALUES = 8
DOWN_VALUES = 2
SECTORS = 16
BLOCK = 128
HALF = 64
MESH = pl.DeviceIdType.MESH

UP_CHARGE = (0, 1, 0, 1)
DOWN_CHARGE = (0, 0, 1, 1)
PHYS_ORDER = (0, 2, 1, 3)
INIT_ROUTES = ((0, 0, (0,)), (2, 0, (1, 3)), (6, 0, (2,)), (3, 1, (0, 3)), (7, 1, (1, 2)))


def role_of(op):
    y = op // 4
    return (op // 2) % 2 * 2 + y % 2, y // 2, op % 2


def op_of(group, down, half):
    return (down * 2 + group % 2) * 4 + group // 2 * 2 + half


def bond_of(group, member):
    return op_of(group, member // 2, member % 2)


def kernel(charge, sizes, coeff, env, mps, proj, out,
           slot, lbuf, mb, own, sib_s, sib_r, part_s, part_r, sbuf, obuf, env_r, mrows, pcols,
           slot_sem, next_ss, init_ss, sib_ss, sib_rs, part_ss, part_rs, out_ss, out_ls, load_sem, out_rs):
    i = lax.axis_index("chain")
    op = lax.axis_index("op")
    g, d, k = role_of(op)
    me = d * 2 + k
    f32, bf16 = jnp.float32, jnp.bfloat16

    bar = pltpu.get_barrier_semaphore()

    def near(step, flip, half):
        z = (op // 2) % 2
        z = 1 - z if flip else z
        return (op // 4 + step) % 4 * 4 + z * 2 + half

    def greet(chain, group, down, half):
        pl.semaphore_signal(bar, inc=1, device_id=(chain, op_of(group, down, half)), device_id_type=MESH)

    @pl.when(i > 0)
    def _():
        for j in range(4):
            greet(i - 1, (g + j) % 4, d, k)

    @pl.when(i == 0)
    def _():
        for source, flip, steps in INIT_ROUTES:
            for step in steps:
                for half in range(2):
                    if source or step:
                        pl.semaphore_signal(
                            bar, inc=1, device_id=(source, near(4 - step, flip, half)), device_id_type=MESH)
    greet(i, g, d, 1 - k)
    greet(i, g, 1 - d, k)
    greet(i, g, 1 - d, 1 - k)

    spreads = (i == 0) | (i == 2) | (i == 3) | (i > 5)

    @pl.when(spreads)
    def _():
        for down in range(2):
            for half in range(2):
                for side in range(2):
                    pltpu.make_async_copy(
                        env.at[:, down, half, :, side], env_r.at[down, half, :, :, :, pl.ds(side * BLOCK, BLOCK)],
                        load_sem.at[0]).start()

    def mps_load(p):
        up = UP_CHARGE[p]
        return pltpu.make_async_copy(
            mps.at[p, pl.ds(0, UP_VALUES - up), d], mrows.at[pl.ds(up, UP_VALUES - up), p // 2, up], load_sem.at[1 + p])

    def proj_load(t):
        up, down = UP_CHARGE[t], DOWN_CHARGE[t]
        return pltpu.make_async_copy(
            proj.at[t, pl.ds(0, UP_VALUES - up), pl.ds(0, DOWN_VALUES - down), pl.ds(k * HALF, HALF)],
            pcols.at[pl.ds(up, UP_VALUES - up), pl.ds(down, DOWN_VALUES - down), t], load_sem.at[5 + t])
    for p in range(4):
        mps_load(p).start()
        proj_load(p).start()
    for count, sites in ((7, (0, 1, 4, 5, 7)), (11, (2, 3)), (9, (6,))):
        here = i == sites[0]
        for other in sites[1:]:
            here = here | (i == other)

        @pl.when(here)
        def _():
            pl.semaphore_wait(bar, count)

    place = g * 4 + me

    @pl.when(spreads)
    def _():
        pltpu.make_async_copy(env_r, env_r, load_sem.at[0]).wait()

    def init_sent(u, count):
        part = slot.at[u, :, pl.ds(0, count)]
        pltpu.make_async_copy(part, part, init_ss.at[u]).wait()

    def spread(first, last):
        for source, flip, steps in INIT_ROUTES:
            def init_row(u, _):
                if source and first:
                    init_sent(u - 2, 2 * len(steps))
                for step in steps:
                    down = (op // 4 + step) % 4 // 2
                    for half in range(2):
                        copy = pltpu.make_async_remote_copy(
                            env_r.at[down, half, u], slot.at[u, :, place], init_ss.at[u], slot_sem.at[u],
                            device_id=(0, near(step, flip, half)), device_id_type=MESH)
                        if source or step:
                            copy.start()
                        else:
                            @pl.when(half != k)
                            def _():
                                copy.start()
                if source == 0:
                    pltpu.make_async_copy(env_r.at[d, k, u], slot.at[u, :, place], slot_sem.at[u]).start()
                return 0

            @pl.when(i == source)
            def _():
                lax.fori_loop(first, last, init_row, 0)
                if source and first:
                    init_sent(UP_VALUES - 2, 2 * len(steps))
                    init_sent(UP_VALUES - 1, 2 * len(steps))

    spread(0, 2)
    zero = jnp.zeros((HALF, BLOCK), bf16)
    for t in range(4):
        pcols[UP_VALUES, 0, t] = zero
        for down in range(2):
            if UP_CHARGE[t]:
                pcols[0, down, t] = zero
        if DOWN_CHARGE[t]:
            for up in range(UP_CHARGE[t], UP_VALUES):
                pcols[up, 0, t] = zero
    for plane in range(2):
        mrows[0, plane, 1] = jnp.zeros((BLOCK, BLOCK), bf16)
    lbuf[2] = jnp.zeros((2, 1024, BLOCK), bf16)

    rows = lax.broadcasted_iota(jnp.int32, (16, 64), 0)
    cols = lax.broadcasted_iota(jnp.int32, (16, 64), 1)
    pick = jnp.where(cols == bond_of(g, rows // 4) * 4 + rows % 4, 1.0, 0.0).astype(bf16)
    mine = lax.dot_general(pick, coeff[...], (((1,), (1,)), ((), ())), preferred_element_type=f32).astype(bf16)
    rows = lax.broadcasted_iota(jnp.int32, (16, 256), 0)
    cols = lax.broadcasted_iota(jnp.int32, (16, 256), 1)
    col_up = jnp.zeros((16, 256), jnp.int32)
    col_down = jnp.zeros((16, 256), jnp.int32)
    row_up = -(rows % 2)
    row_down = -((rows // 2) % 2)
    for n in range(16):
        b = bond_of(n // 4, n % 4)
        col_up = jnp.where(cols // 16 == n, charge[b, 0], col_up)
        col_down = jnp.where(cols // 16 == n, charge[b, 1], col_down)
    for m in range(4):
        b = bond_of(g, m)
        row_up = row_up + jnp.where(rows // 4 == m, charge[b, 0], 0)
        row_down = row_down + jnp.where(rows // 4 == m, charge[b, 1], 0)
    rows = lax.broadcasted_iota(jnp.int32, (64, 256), 0)
    cols = lax.broadcasted_iota(jnp.int32, (64, 256), 1)
    slot_bond = bond_of(cols // 64, cols // 16 % 4)
    long_rows = lax.broadcasted_iota(jnp.int32, (256, 256), 0)
    long_cols = lax.broadcasted_iota(jnp.int32, (256, 256), 1)
    repeat = jnp.where(
        lax.broadcasted_iota(jnp.int32, (256, 16), 0) // 16 == lax.broadcasted_iota(jnp.int32, (256, 16), 1),
        1.0, 0.0).astype(bf16)
    for rank, p in enumerate(PHYS_ORDER):
        widen = jnp.where(rows == slot_bond * 4 + p, 1.0, 0.0).astype(bf16)
        wide = jnp.dot(mine, widen, preferred_element_type=f32)
        match = (col_up == row_up + UP_CHARGE[p]) & (col_down == row_down + DOWN_CHARGE[p])
        wide = jnp.where(match, wide, 0.0).astype(bf16)
        tall = jnp.dot(repeat, wide, preferred_element_type=f32)
        mb[rank * 256:(rank + 1) * 256, :] = jnp.where(long_rows % 16 == long_cols % 16, tall, 0.0).astype(bf16)

    for p in range(4):
        mps_load(p).wait()
    rows = lax.broadcasted_iota(jnp.int32, (BLOCK, BLOCK), 0)
    cols = lax.broadcasted_iota(jnp.int32, (BLOCK, BLOCK), 1)

    def mask_row(u, _):
        for plane in range(2):
            for up in range(2):
                left = sizes[i, jnp.maximum(u - up, 0) * 2 + d]
                right = sizes[i + 1, u * 2 + jnp.minimum(d + plane, 1)]
                keep = (rows < left) & (cols < right)
                mrows[u, plane, up] = jnp.where(keep, mrows[u, plane, up].astype(f32), 0.0).astype(bf16)
        return 0
    lax.fori_loop(0, UP_VALUES, mask_row, 0)
    for t in range(4):
        proj_load(t).wait()
    spread(2, UP_VALUES)

    def mix(u, first):
        place = first * (1 + u % 2)
        for pair in range(2):
            x = slot[u, pair].reshape(256, 256)
            y = jnp.dot(mb[pl.ds(pl.multiple_of(first * 512, 512), 512), :], x, preferred_element_type=f32).astype(bf16)
            for side in range(2):
                for plane in range(2):
                    lbuf[place, plane, pl.ds((2 * pair + side) * 256, 256)] = (
                        y[plane * 256:(plane + 1) * 256, side * BLOCK:(side + 1) * BLOCK])

    def apply(u, plane):
        both = jnp.concatenate([lbuf[0, plane], lbuf[1 + (u + 1) % 2, plane]], axis=1)
        grown = jnp.dot(both, mrows[u, plane].reshape(256, BLOCK), preferred_element_type=f32).astype(bf16)
        for m in range(4):
            b = bond_of(g, m)
            up = u + charge[b, 0]
            down = d + plane + charge[b, 1]
            inside = (up >= 0) & (up < UP_VALUES) & (down >= 0) & (down < DOWN_VALUES)
            up = jnp.where(inside, up, UP_VALUES)
            down = jnp.where(inside, down, 0)
            piece = jnp.concatenate(
                [grown[at * 256 + m * 64 + t * 16:at * 256 + m * 64 + t * 16 + 16] for t in range(4) for at in range(4)], axis=0)
            res = lax.dot_general(pcols[up, down].reshape(256, BLOCK), piece, (((0,), (0,)), ((), ())),
                                  preferred_element_type=f32)
            own[plane, m] = jnp.where(k == 0, res[:HALF], res[HALF:])
            sib_s[u, plane, m] = jnp.where(k == 0, res[HALF:], res[:HALF]).astype(bf16)

    def sibling(u, plane):
        return pltpu.make_async_remote_copy(
            sib_s.at[u, plane], sib_r.at[u, plane], sib_ss.at[u, plane], sib_rs.at[u, plane],
            device_id=(i, op_of(g, d, 1 - k)), device_id_type=MESH)

    def partial(u):
        return pltpu.make_async_remote_copy(
            part_s.at[u], part_r.at[u], part_ss.at[u], part_rs.at[u],
            device_id=(i, op_of(g, 1 - d, k)), device_id_type=MESH)

    def to_next(u, group):
        return pltpu.make_async_remote_copy(
            sbuf.at[u], slot.at[u, :, pl.ds(g * 4, 4)], next_ss.at[u], slot_sem.at[u],
            device_id=(i + 1, op_of(group, d, k)), device_id_type=MESH)

    def hand_over(u):
        sibling(u, 1).wait_recv()
        for m in range(4):
            part_s[u, m] = (own[1, m] + sib_r[u, 1, m].astype(f32)).astype(bf16)
        partial(u).start()

    def give(u, _):
        for j in range(1, 4):
            m = (me + j) % 4
            pltpu.make_async_remote_copy(
                obuf.at[m, u], out.at[u, d, k], out_ss.at[u], out_rs,
                device_id=(i, bond_of(g, m)), device_id_type=MESH).start()
        pltpu.make_async_copy(obuf.at[me, u], out.at[u, d, k], out_ls.at[u]).start()
        return 0

    def finish(u):
        sibling(u, 0).wait_recv()

        @pl.when(d == 1)
        def _():
            partial(u).wait_recv()
            for m in range(4):
                own[0, m] = own[0, m] + part_r[u, m].astype(f32)

        for m in range(4):
            res = (own[0, m] + sib_r[u, 0, m].astype(f32)).astype(bf16)
            obuf[m, u] = res
            for pair in range(2):
                for side in range(2):
                    start = pair * 32 + side * 16
                    sbuf[u, pair, m, :, pl.ds(side * BLOCK, BLOCK)] = res[start:start + 16]

        @pl.when(i < 7)
        def _():
            for flip_z, flip_y in ((1, 1), (0, 1), (1, 0), (0, 0)):
                z = g // 2 + flip_z * (1 - 2 * (g // 2))
                y = g % 2 + flip_y * (1 - 2 * (g % 2))
                to_next(u, z * 2 + y).start()

        @pl.when((i == 7) | ((i == 6) & (u < 4)))
        def _():
            give(u, 0)

    def step(n, _):
        u, plane = n // 2, n % 2

        @pl.when(plane == 0)
        def _():
            pltpu.make_async_copy(slot.at[u], slot.at[u], slot_sem.at[u]).wait()

        @pl.when(n < 2 * UP_VALUES - 1)
        def _():
            mix(u, plane)

        @pl.when((plane == 0) | (d == 0))
        def _():
            apply(u, plane)
            sibling(u, plane).start()

        @pl.when(plane == 0)
        def _():
            finish(u)

        @pl.when((plane == 1) & (d == 0))
        def _():
            hand_over(u)
        return 0

    lax.fori_loop(0, 2 * UP_VALUES, step, 0)

    @pl.when(i == 6)
    def _():
        lax.fori_loop(4, UP_VALUES, give, 0)

    @pl.when(i < 6)
    def _():
        for j in range(1, 4):
            m = (me + j) % 4
            pltpu.make_async_remote_copy(
                obuf.at[m], out.at[:, d, k], out_ss.at[0], out_rs,
                device_id=(i, bond_of(g, m)), device_id_type=MESH).start()
        pltpu.make_async_copy(obuf.at[me], out.at[:, d, k], out_ls.at[0]).start()
        pltpu.make_async_copy(obuf.at[pl.ds(0, 3)], obuf.at[pl.ds(0, 3)], out_ss.at[0]).wait()
        pltpu.make_async_copy(obuf.at[0], obuf.at[0], out_ls.at[0]).wait()

    def drain(u, _):
        @pl.when(i == 0)
        def _():
            init_sent(u, 1)

        @pl.when(i < 7)
        def _():
            pltpu.make_async_copy(slot.at[u], slot.at[u], next_ss.at[u]).wait()
        sibling(u, 0).wait_send()

        @pl.when(d == 0)
        def _():
            sibling(u, 1).wait_send()
            partial(u).wait_send()

        @pl.when(i > 5)
        def _():
            three = obuf.at[pl.ds(0, 3), u]
            pltpu.make_async_copy(three, three, out_ss.at[u]).wait()
            pltpu.make_async_copy(obuf.at[0, u], obuf.at[0, u], out_ls.at[u]).wait()
        return 0

    lax.fori_loop(0, UP_VALUES, drain, 0)
    pltpu.make_async_copy(out.at[pl.ds(0, 6)], out.at[pl.ds(0, 6)], out_rs).wait()


def on_device(env_in, mps, proj, mpo, mpo_charge, block_sizes):
    bf16 = jnp.bfloat16
    vm = pl.BlockSpec(memory_space=pltpu.VMEM)
    sm = pl.BlockSpec(memory_space=pltpu.SMEM)
    hbm = pl.BlockSpec(memory_space=pltpu.HBM)
    dma = pltpu.SemaphoreType.DMA
    out = pl.pallas_call(
        kernel,
        out_shape=jax.ShapeDtypeStruct((UP_VALUES, DOWN_VALUES, 2, HALF, BLOCK), bf16),
        in_specs=[sm, sm, vm, hbm, hbm, hbm],
        out_specs=hbm,
        scratch_shapes=[
            pltpu.VMEM((UP_VALUES, 2, 16, 16, 256), bf16),
            pltpu.VMEM((3, 2, 1024, BLOCK), bf16),
            pltpu.VMEM((1024, 256), bf16),
            pltpu.VMEM((2, 4, HALF, BLOCK), jnp.float32),
            pltpu.VMEM((UP_VALUES, 2, 4, HALF, BLOCK), bf16),
            pltpu.VMEM((UP_VALUES, 2, 4, HALF, BLOCK), bf16),
            pltpu.VMEM((UP_VALUES, 4, HALF, BLOCK), bf16),
            pltpu.VMEM((UP_VALUES, 4, HALF, BLOCK), bf16),
            pltpu.VMEM((UP_VALUES, 2, 4, 16, 256), bf16),
            pltpu.VMEM((4, UP_VALUES, HALF, BLOCK), bf16),
            pltpu.VMEM((2, 2, UP_VALUES, 2, 16, 256), bf16),
            pltpu.VMEM((UP_VALUES, 2, 2, BLOCK, BLOCK), bf16),
            pltpu.VMEM((UP_VALUES + 1, 2, 4, HALF, BLOCK), bf16),
            dma((8,)), dma((8,)), dma((8,)), dma((8, 2)), dma((8, 2)), dma((8,)), dma((8,)), dma((8,)), dma((8,)),
            dma((9,)), dma,
        ],
        compiler_params=pltpu.CompilerParams(collective_id=0, has_side_effects=True, vmem_limit_bytes=53 << 20),
        name="sweep",
    )(
        mpo_charge, block_sizes, mpo.reshape(64, 64),
        env_in.reshape(UP_VALUES, 2, 2, 2, 2, 16, BLOCK),
        mps.reshape(4, UP_VALUES, DOWN_VALUES, BLOCK, BLOCK),
        proj.reshape(4, UP_VALUES, DOWN_VALUES, BLOCK, BLOCK),
    )
    return out.reshape(1, 1, SECTORS, BLOCK, BLOCK)


def solution(mesh):
    return jax.shard_map(
        on_device,
        mesh=mesh,
        in_specs=(
            P("op", None, None, None),
            P("chain", None, None, None, None),
            P("chain", None, None, None, None),
            P("chain", None, None, None, None),
            P(),
            P(),
        ),
        out_specs=P("chain", "op", None, None, None),
        check_vma=False,
    )
```

```python
import jax
import jax.numpy as jnp
from jax import lax
from jax.experimental import pallas as pl
from jax.experimental.pallas import tpu as pltpu
from jax.sharding import PartitionSpec as P

UP_VALUES = 8
DOWN_VALUES = 2
SECTORS = 16
BLOCK = 128
HALF = 64
MESH = pl.DeviceIdType.MESH

UP_CHARGE = (0, 1, 0, 1)
DOWN_CHARGE = (0, 0, 1, 1)
PHYS_ORDER = (0, 2, 1, 3)
INIT_ROUTES = ((0, 0, (0,)), (2, 0, (1, 3)), (6, 0, (2,)), (3, 1, (0, 3)), (7, 1, (1, 2)))


def role_of(op):
    y = op // 4
    return (op // 2) % 2 * 2 + y % 2, y // 2, op % 2


def op_of(group, down, half):
    return (down * 2 + group % 2) * 4 + group // 2 * 2 + half


def bond_of(group, member):
    return op_of(group, member // 2, member % 2)


def kernel(charge, sizes, coeff, env, mps, proj, out,
           slot, lbuf, mb, own, sib_s, sib_r, part_s, part_r, sbuf, obuf, env_r, mrows, pcols,
           slot_sem, next_ss, init_ss, sib_ss, sib_rs, part_ss, part_rs, out_ss, out_ls, load_sem, out_rs):
    i = lax.axis_index("chain")
    op = lax.axis_index("op")
    g, d, k = role_of(op)
    me = d * 2 + k
    f32, bf16 = jnp.float32, jnp.bfloat16

    bar = pltpu.get_barrier_semaphore()

    def near(step, flip, half):
        z = (op // 2) % 2
        z = 1 - z if flip else z
        return (op // 4 + step) % 4 * 4 + z * 2 + half

    def greet(chain, group, down, half):
        pl.semaphore_signal(bar, inc=1, device_id=(chain, op_of(group, down, half)), device_id_type=MESH)

    @pl.when(i > 0)
    def _():
        for j in range(4):
            greet(i - 1, (g + j) % 4, d, k)

    @pl.when(i == 0)
    def _():
        for source, flip, steps in INIT_ROUTES:
            for step in steps:
                for half in range(2):
                    if source or step:
                        pl.semaphore_signal(
                            bar, inc=1, device_id=(source, near(4 - step, flip, half)), device_id_type=MESH)
    greet(i, g, d, 1 - k)
    greet(i, g, 1 - d, k)
    greet(i, g, 1 - d, 1 - k)

    spreads = (i == 0) | (i == 2) | (i == 3) | (i > 5)

    @pl.when(spreads)
    def _():
        for down in range(2):
            for half in range(2):
                for side in range(2):
                    pltpu.make_async_copy(
                        env.at[:, down, half, :, side], env_r.at[down, half, :, :, :, pl.ds(side * BLOCK, BLOCK)],
                        load_sem.at[0]).start()

    def mps_load(p):
        up = UP_CHARGE[p]
        return pltpu.make_async_copy(
            mps.at[p, pl.ds(0, UP_VALUES - up), d], mrows.at[pl.ds(up, UP_VALUES - up), p // 2, up], load_sem.at[1 + p])

    def proj_load(t):
        up, down = UP_CHARGE[t], DOWN_CHARGE[t]
        return pltpu.make_async_copy(
            proj.at[t, pl.ds(0, UP_VALUES - up), pl.ds(0, DOWN_VALUES - down), pl.ds(k * HALF, HALF)],
            pcols.at[pl.ds(up, UP_VALUES - up), pl.ds(down, DOWN_VALUES - down), t], load_sem.at[5 + t])
    for p in range(4):
        mps_load(p).start()
        proj_load(p).start()
    for count, sites in ((7, (0, 1, 4, 5, 7)), (11, (2, 3)), (9, (6,))):
        here = i == sites[0]
        for other in sites[1:]:
            here = here | (i == other)

        @pl.when(here)
        def _():
            pl.semaphore_wait(bar, count)

    place = g * 4 + me

    @pl.when(spreads)
    def _():
        pltpu.make_async_copy(env_r, env_r, load_sem.at[0]).wait()

    def init_sent(u, count):
        part = slot.at[u, :, pl.ds(0, count)]
        pltpu.make_async_copy(part, part, init_ss.at[u]).wait()

    def spread(first, last):
        for source, flip, steps in INIT_ROUTES:
            def init_row(u, _):
                if source and first:
                    init_sent(u - 2, 2 * len(steps))
                for step in steps:
                    down = (op // 4 + step) % 4 // 2
                    for half in range(2):
                        copy = pltpu.make_async_remote_copy(
                            env_r.at[down, half, u], slot.at[u, :, place], init_ss.at[u], slot_sem.at[u],
                            device_id=(0, near(step, flip, half)), device_id_type=MESH)
                        if source or step:
                            copy.start()
                        else:
                            @pl.when(half != k)
                            def _():
                                copy.start()
                if source == 0:
                    pltpu.make_async_copy(env_r.at[d, k, u], slot.at[u, :, place], slot_sem.at[u]).start()
                return 0

            @pl.when(i == source)
            def _():
                lax.fori_loop(first, last, init_row, 0)
                if source and first:
                    init_sent(UP_VALUES - 2, 2 * len(steps))
                    init_sent(UP_VALUES - 1, 2 * len(steps))

    spread(0, 2)
    zero = jnp.zeros((HALF, BLOCK), bf16)
    for t in range(4):
        pcols[UP_VALUES, 0, t] = zero
        for down in range(2):
            if UP_CHARGE[t]:
                pcols[0, down, t] = zero
        if DOWN_CHARGE[t]:
            for up in range(UP_CHARGE[t], UP_VALUES):
                pcols[up, 0, t] = zero
    for plane in range(2):
        mrows[0, plane, 1] = jnp.zeros((BLOCK, BLOCK), bf16)
    lbuf[2] = jnp.zeros((2, 1024, BLOCK), bf16)

    rows = lax.broadcasted_iota(jnp.int32, (16, 64), 0)
    cols = lax.broadcasted_iota(jnp.int32, (16, 64), 1)
    pick = jnp.where(cols == bond_of(g, rows // 4) * 4 + rows % 4, 1.0, 0.0).astype(bf16)
    mine = lax.dot_general(pick, coeff[...], (((1,), (1,)), ((), ())), preferred_element_type=f32).astype(bf16)
    rows = lax.broadcasted_iota(jnp.int32, (16, 256), 0)
    cols = lax.broadcasted_iota(jnp.int32, (16, 256), 1)
    col_up = jnp.zeros((16, 256), jnp.int32)
    col_down = jnp.zeros((16, 256), jnp.int32)
    row_up = -(rows % 2)
    row_down = -((rows // 2) % 2)
    for n in range(16):
        b = bond_of(n // 4, n % 4)
        col_up = jnp.where(cols // 16 == n, charge[b, 0], col_up)
        col_down = jnp.where(cols // 16 == n, charge[b, 1], col_down)
    for m in range(4):
        b = bond_of(g, m)
        row_up = row_up + jnp.where(rows // 4 == m, charge[b, 0], 0)
        row_down = row_down + jnp.where(rows // 4 == m, charge[b, 1], 0)
    rows = lax.broadcasted_iota(jnp.int32, (64, 256), 0)
    cols = lax.broadcasted_iota(jnp.int32, (64, 256), 1)
    slot_bond = bond_of(cols // 64, cols // 16 % 4)
    long_rows = lax.broadcasted_iota(jnp.int32, (256, 256), 0)
    long_cols = lax.broadcasted_iota(jnp.int32, (256, 256), 1)
    repeat = jnp.where(
        lax.broadcasted_iota(jnp.int32, (256, 16), 0) // 16 == lax.broadcasted_iota(jnp.int32, (256, 16), 1),
        1.0, 0.0).astype(bf16)
    for rank, p in enumerate(PHYS_ORDER):
        widen = jnp.where(rows == slot_bond * 4 + p, 1.0, 0.0).astype(bf16)
        wide = jnp.dot(mine, widen, preferred_element_type=f32)
        match = (col_up == row_up + UP_CHARGE[p]) & (col_down == row_down + DOWN_CHARGE[p])
        wide = jnp.where(match, wide, 0.0).astype(bf16)
        tall = jnp.dot(repeat, wide, preferred_element_type=f32)
        mb[rank * 256:(rank + 1) * 256, :] = jnp.where(long_rows % 16 == long_cols % 16, tall, 0.0).astype(bf16)

    for p in range(4):
        mps_load(p).wait()
    rows = lax.broadcasted_iota(jnp.int32, (BLOCK, BLOCK), 0)
    cols = lax.broadcasted_iota(jnp.int32, (BLOCK, BLOCK), 1)

    def mask_row(u, _):
        for plane in range(2):
            for up in range(2):
                left = sizes[i, jnp.maximum(u - up, 0) * 2 + d]
                right = sizes[i + 1, u * 2 + jnp.minimum(d + plane, 1)]
                keep = (rows < left) & (cols < right)
                mrows[u, plane, up] = jnp.where(keep, mrows[u, plane, up].astype(f32), 0.0).astype(bf16)
        return 0
    lax.fori_loop(0, UP_VALUES, mask_row, 0)
    for t in range(4):
        proj_load(t).wait()
    spread(2, UP_VALUES)

    def mix(u, first):
        place = first * (1 + u % 2)
        for pair in range(2):
            x = slot[u, pair].reshape(256, 256)
            y = jnp.dot(mb[pl.ds(pl.multiple_of(first * 512, 512), 512), :], x, preferred_element_type=f32).astype(bf16)
            for side in range(2):
                for plane in range(2):
                    lbuf[place, plane, pl.ds((2 * pair + side) * 256, 256)] = (
                        y[plane * 256:(plane + 1) * 256, side * BLOCK:(side + 1) * BLOCK])

    def apply(u, plane):
        both = jnp.concatenate([lbuf[0, plane], lbuf[1 + (u + 1) % 2, plane]], axis=1)
        grown = jnp.dot(both, mrows[u, plane].reshape(256, BLOCK), preferred_element_type=f32).astype(bf16)
        for m in range(4):
            b = bond_of(g, m)
            up = u + charge[b, 0]
            down = d + plane + charge[b, 1]
            inside = (up >= 0) & (up < UP_VALUES) & (down >= 0) & (down < DOWN_VALUES)
            up = jnp.where(inside, up, UP_VALUES)
            down = jnp.where(inside, down, 0)
            piece = jnp.concatenate(
                [grown[at * 256 + m * 64 + t * 16:at * 256 + m * 64 + t * 16 + 16] for t in range(4) for at in range(4)], axis=0)
            res = lax.dot_general(pcols[up, down].reshape(256, BLOCK), piece, (((0,), (0,)), ((), ())),
                                  preferred_element_type=f32)
            own[plane, m] = jnp.where(k == 0, res[:HALF], res[HALF:])
            sib_s[u, plane, m] = jnp.where(k == 0, res[HALF:], res[:HALF]).astype(bf16)

    def sibling(u, plane):
        return pltpu.make_async_remote_copy(
            sib_s.at[u, plane], sib_r.at[u, plane], sib_ss.at[u, plane], sib_rs.at[u, plane],
            device_id=(i, op_of(g, d, 1 - k)), device_id_type=MESH)

    def partial(u):
        return pltpu.make_async_remote_copy(
            part_s.at[u], part_r.at[u], part_ss.at[u], part_rs.at[u],
            device_id=(i, op_of(g, 1 - d, k)), device_id_type=MESH)

    def to_next(u, group):
        return pltpu.make_async_remote_copy(
            sbuf.at[u], slot.at[u, :, pl.ds(g * 4, 4)], next_ss.at[u], slot_sem.at[u],
            device_id=(i + 1, op_of(group, d, k)), device_id_type=MESH)

    def hand_over(u):
        sibling(u, 1).wait_recv()
        for m in range(4):
            part_s[u, m] = (own[1, m] + sib_r[u, 1, m].astype(f32)).astype(bf16)
        partial(u).start()

    def finish(u):
        sibling(u, 0).wait_recv()

        @pl.when(d == 1)
        def _():
            partial(u).wait_recv()
            for m in range(4):
                own[0, m] = own[0, m] + part_r[u, m].astype(f32)

        for m in range(4):
            res = (own[0, m] + sib_r[u, 0, m].astype(f32)).astype(bf16)
            obuf[m, u] = res
            for pair in range(2):
                for side in range(2):
                    start = pair * 32 + side * 16
                    sbuf[u, pair, m, :, pl.ds(side * BLOCK, BLOCK)] = res[start:start + 16]

        @pl.when(i < 7)
        def _():
            for flip_z, flip_y in ((1, 1), (0, 1), (1, 0), (0, 0)):
                z = (g // 2 + flip_z + k) % 2
                y = g % 2 + flip_y * (1 - 2 * (g % 2))
                to_next(u, z * 2 + y).start()

        @pl.when(i > 5)
        def _():
            for j in range(1, 4):
                m = (me + j) % 4
                pltpu.make_async_remote_copy(
                    obuf.at[m, u], out.at[u, d, k], out_ss.at[u], out_rs,
                    device_id=(i, bond_of(g, m)), device_id_type=MESH).start()
            pltpu.make_async_copy(obuf.at[me, u], out.at[u, d, k], out_ls.at[u]).start()

    def step(n, _):
        u, plane = n // 2, n % 2

        @pl.when(plane == 0)
        def _():
            pltpu.make_async_copy(slot.at[u], slot.at[u], slot_sem.at[u]).wait()

        @pl.when(n < 2 * UP_VALUES - 1)
        def _():
            mix(u, plane)

        @pl.when((plane == 0) | (d == 0))
        def _():
            apply(u, plane)
            sibling(u, plane).start()

        @pl.when(plane == 0)
        def _():
            finish(u)

        @pl.when((plane == 1) & (d == 0))
        def _():
            hand_over(u)
        return 0

    lax.fori_loop(0, 2 * UP_VALUES, step, 0)

    @pl.when(i < 6)
    def _():
        for j in range(1, 4):
            m = (me + j) % 4
            pltpu.make_async_remote_copy(
                obuf.at[m], out.at[:, d, k], out_ss.at[0], out_rs,
                device_id=(i, bond_of(g, m)), device_id_type=MESH).start()
        pltpu.make_async_copy(obuf.at[me], out.at[:, d, k], out_ls.at[0]).start()
        pltpu.make_async_copy(obuf.at[pl.ds(0, 3)], obuf.at[pl.ds(0, 3)], out_ss.at[0]).wait()
        pltpu.make_async_copy(obuf.at[0], obuf.at[0], out_ls.at[0]).wait()

    def drain(u, _):
        @pl.when(i == 0)
        def _():
            init_sent(u, 1)

        @pl.when(i < 7)
        def _():
            pltpu.make_async_copy(slot.at[u], slot.at[u], next_ss.at[u]).wait()
        sibling(u, 0).wait_send()

        @pl.when(d == 0)
        def _():
            sibling(u, 1).wait_send()
            partial(u).wait_send()

        @pl.when(i > 5)
        def _():
            three = obuf.at[pl.ds(0, 3), u]
            pltpu.make_async_copy(three, three, out_ss.at[u]).wait()
            pltpu.make_async_copy(obuf.at[0, u], obuf.at[0, u], out_ls.at[u]).wait()
        return 0

    lax.fori_loop(0, UP_VALUES, drain, 0)
    pltpu.make_async_copy(out.at[pl.ds(0, 6)], out.at[pl.ds(0, 6)], out_rs).wait()


def on_device(env_in, mps, proj, mpo, mpo_charge, block_sizes):
    bf16 = jnp.bfloat16
    vm = pl.BlockSpec(memory_space=pltpu.VMEM)
    sm = pl.BlockSpec(memory_space=pltpu.SMEM)
    hbm = pl.BlockSpec(memory_space=pltpu.HBM)
    dma = pltpu.SemaphoreType.DMA
    out = pl.pallas_call(
        kernel,
        out_shape=jax.ShapeDtypeStruct((UP_VALUES, DOWN_VALUES, 2, HALF, BLOCK), bf16),
        in_specs=[sm, sm, vm, hbm, hbm, hbm],
        out_specs=hbm,
        scratch_shapes=[
            pltpu.VMEM((UP_VALUES, 2, 16, 16, 256), bf16),
            pltpu.VMEM((3, 2, 1024, BLOCK), bf16),
            pltpu.VMEM((1024, 256), bf16),
            pltpu.VMEM((2, 4, HALF, BLOCK), jnp.float32),
            pltpu.VMEM((UP_VALUES, 2, 4, HALF, BLOCK), bf16),
            pltpu.VMEM((UP_VALUES, 2, 4, HALF, BLOCK), bf16),
            pltpu.VMEM((UP_VALUES, 4, HALF, BLOCK), bf16),
            pltpu.VMEM((UP_VALUES, 4, HALF, BLOCK), bf16),
            pltpu.VMEM((UP_VALUES, 2, 4, 16, 256), bf16),
            pltpu.VMEM((4, UP_VALUES, HALF, BLOCK), bf16),
            pltpu.VMEM((2, 2, UP_VALUES, 2, 16, 256), bf16),
            pltpu.VMEM((UP_VALUES, 2, 2, BLOCK, BLOCK), bf16),
            pltpu.VMEM((UP_VALUES + 1, 2, 4, HALF, BLOCK), bf16),
            dma((8,)), dma((8,)), dma((8,)), dma((8, 2)), dma((8, 2)), dma((8,)), dma((8,)), dma((8,)), dma((8,)),
            dma((9,)), dma,
        ],
        compiler_params=pltpu.CompilerParams(collective_id=0, has_side_effects=True, vmem_limit_bytes=53 << 20),
        name="sweep",
    )(
        mpo_charge, block_sizes, mpo.reshape(64, 64),
        env_in.reshape(UP_VALUES, 2, 2, 2, 2, 16, BLOCK),
        mps.reshape(4, UP_VALUES, DOWN_VALUES, BLOCK, BLOCK),
        proj.reshape(4, UP_VALUES, DOWN_VALUES, BLOCK, BLOCK),
    )
    return out.reshape(1, 1, SECTORS, BLOCK, BLOCK)


def solution(mesh):
    return jax.shard_map(
        on_device,
        mesh=mesh,
        in_specs=(
            P("op", None, None, None),
            P("chain", None, None, None, None),
            P("chain", None, None, None, None),
            P("chain", None, None, None, None),
            P(),
            P(),
        ),
        out_specs=P("chain", "op", None, None, None),
        check_vma=False,
    )
```
